256 devices in a mesh: seq: 128 (over z, y, x_lo, core), head: 2 (over x_hi).
Axes of the slice: x: 4 (x_hi: 2, x_lo: 2; x = x_hi * 2 + x_lo), y: 4, z: 8, core: 2. Of those that a mesh axis runs over, the one named last changes fastest.
Arguments:
- events: bfloat16 [16, 32768, 512], P(None, ('seq', 'head')), may hold values from -6 to 6
- global_tokens: bfloat16 [16, 128, 512], P(None, 'seq'), may hold values from -6 to 6
- lengths: int32 [16], replicated, may hold values from 8 to 32768, as said below
- inner_qkv: bfloat16 [512, 1536], replicated, may hold values from -0.26516504 to 0.26516504
- inner_out: bfloat16 [512, 512], replicated, may hold values from -0.25 to 0.25
- merge_gain: float32 [512], replicated, may hold values from 0.25 to 1.75
- global_gain: float32 [512], replicated, may hold values from 0.25 to 1.75
- mixed_qkv: bfloat16 [512, 1536], replicated, may hold values from -0.26516504 to 0.26516504
- mixed_out: bfloat16 [512, 512], replicated, may hold values from -1.5 to 1.5
Outputs:
- merged_out: bfloat16 [16, 4096, 512], P(None, ('seq', 'head'))
- global_heads: bfloat16 [128, 2, 4096], P('seq', 'head')
The draws below stay inside these ranges and needn't reach their ends.
Inputs may be any that keep to these rules, and one draw needn't show every extreme that they name: `lengths`: each length is a multiple of 8; some user has the full 32768 events.
All inputs are finite; a program needn't handle non-finite values.
Results may differ from the reference program's by a relative error of at most 0.025.
Values may be sent and summed in bfloat16 or wider, within the bound.
No kernel may reach another device: no remote copies, remote signals or barrier semaphores. Data moves between devices by JAX's collectives and lax.ppermute only.
A program may use at most 128 MiB of HBM per device.

```python
import jax
import jax.numpy as jnp
from jax import lax

D = 512
HEADS = 16
GLOBALS = 128
USERS = 16
EVENTS = 32768


def draw_events(key, part):
    key = jax.random.fold_in(key, 11)
    return jnp.clip(jax.random.normal(key, (USERS, EVENTS, D), jnp.float32), -6.0, 6.0).astype(jnp.bfloat16)


def draw_global_tokens(key, part):
    key = jax.random.fold_in(key, 23)
    return jnp.clip(jax.random.normal(key, (USERS, GLOBALS, D), jnp.float32), -6.0, 6.0).astype(jnp.bfloat16)


def draw_inner_qkv(key, part):
    key = jax.random.fold_in(key, 13)
    return (jnp.clip(jax.random.normal(key, (D, 3 * D), jnp.float32), -6.0, 6.0) * D ** (-0.5)).astype(jnp.bfloat16)


def draw_mixed_qkv(key, part):
    key = jax.random.fold_in(key, 17)
    return (jnp.clip(jax.random.normal(key, (D, 3 * D), jnp.float32), -6.0, 6.0) * D ** (-0.5)).astype(jnp.bfloat16)


def draw_lengths(key, part):
    key = jax.random.fold_in(key, 7)
    first_key, second_key = jax.random.split(key)
    groups = jax.random.randint(first_key, (USERS,), 1, EVENTS // 8 + 1)
    lengths = groups * 8
    longest = jax.random.randint(second_key, (), 0, USERS)
    lengths = lengths.at[longest].set(EVENTS)
    return lengths.astype(jnp.int32)


def scatter_about(stream_key, shape, deviation, reach, kind=jnp.bfloat16):
    values = jax.random.normal(stream_key, shape, jnp.float32) * deviation
    return jnp.minimum(jnp.maximum(values, -reach), reach).astype(kind)


def setup_inputs(seed: int = 0) -> dict:
    splits = jax.random.split(jax.random.key(seed), 10)
    events = draw_events(jax.random.fold_in(splits[9], 71), 0)
    global_tokens = draw_global_tokens(jax.random.fold_in(splits[9], 71), 0)
    lengths = draw_lengths(jax.random.fold_in(splits[9], 71), 0)
    inner_qkv = draw_inner_qkv(jax.random.fold_in(splits[9], 71), 0)
    inner_out = scatter_about(splits[4], (D, D), D ** -0.5, 0.25)
    merge_gain = jnp.clip(1.0 + 0.15 * jax.random.normal(splits[5], (D,), jnp.float32), 0.25, 1.75)
    global_gain = jnp.clip(1.0 + 0.15 * jax.random.normal(splits[6], (D,), jnp.float32), 0.25, 1.75)
    mixed_qkv = draw_mixed_qkv(jax.random.fold_in(splits[9], 71), 0)
    mixed_out = scatter_about(splits[8], (D, D), (D // (2 * HEADS)) ** -0.5, 1.5)
    return {"events": events, "global_tokens": global_tokens, "lengths": lengths, "inner_qkv": inner_qkv, "inner_out": inner_out, "merge_gain": merge_gain, "global_gain": global_gain, "mixed_qkv": mixed_qkv, "mixed_out": mixed_out}


def softmax_last(scores):
    top = lax.optimization_barrier(jnp.max(scores, axis=-1, keepdims=True))
    expd = jnp.exp(scores - top)
    return expd / lax.optimization_barrier(jnp.sum(expd, axis=-1, keepdims=True))

def norm_rows(values, gain):
    wide = values.astype(jnp.float32)
    scale = lax.rsqrt(lax.optimization_barrier(jnp.mean(wide * wide, axis=-1, keepdims=True)) + 1e-06)
    return (wide * scale * gain).astype(jnp.bfloat16)

def inner_merge(user_events, inner_qkv, inner_out):
    span, width = user_events.shape
    groups = span // 8
    head_dim = width // 8
    flat = jnp.dot(user_events, inner_qkv, preferred_element_type=jnp.float32).astype(jnp.bfloat16)
    flat = flat.reshape(groups, 8, 3, 8, head_dim).astype(jnp.float32)
    scores = jnp.einsum('gqhd,gkhd->ghqk', flat[:, :, 0], flat[:, :, 1], precision=lax.Precision.HIGHEST) / jnp.sqrt(jnp.float32(head_dim))
    pooled_w = lax.optimization_barrier(jnp.mean(softmax_last(scores), axis=2)).astype(jnp.bfloat16)
    pooled = jnp.einsum('ghk,gkhd->ghd', pooled_w.astype(jnp.float32), flat[:, :, 2], precision=lax.Precision.HIGHEST)
    pooled = pooled.astype(jnp.bfloat16).reshape(groups, width)
    mean_events = lax.optimization_barrier(jnp.mean(user_events.reshape(groups, 8, width).astype(jnp.float32), axis=1))
    return (mean_events + jnp.dot(pooled, inner_out, preferred_element_type=jnp.float32)).astype(jnp.bfloat16)

def attend_rows(queries, keys, values, allowed):
    scale = 1.0 / jnp.sqrt(jnp.float32(queries.shape[1]))
    scores = jnp.dot(queries.astype(jnp.float32), keys.astype(jnp.float32).T, precision=lax.Precision.HIGHEST) * scale
    scores = jnp.where(allowed, scores, jnp.float32(-1e+30))
    weights = softmax_last(scores).astype(jnp.bfloat16)
    return jnp.dot(weights.astype(jnp.float32), values.astype(jnp.float32), precision=lax.Precision.HIGHEST).astype(jnp.bfloat16)

def pair_attention(merged_qkv, global_qkv, valid):
    count = merged_qkv.shape[0]
    glob = global_qkv.shape[0]
    head_dim = merged_qkv.shape[1] // 3
    keys = jnp.concatenate([global_qkv[:, head_dim:2 * head_dim], merged_qkv[:, head_dim:2 * head_dim]], axis=0)
    values = jnp.concatenate([global_qkv[:, 2 * head_dim:], merged_qkv[:, 2 * head_dim:]], axis=0)
    columns = jnp.arange(glob + count, dtype=jnp.int32) - glob
    key_live = columns < valid
    glob_out = attend_rows(global_qkv[:, :head_dim], keys, values, key_live[None, :])
    position = jnp.arange(count, dtype=jnp.int32)
    allowed = key_live[None, :] & (columns[None, :] <= position[:, None])
    merged_att = attend_rows(merged_qkv[:, :head_dim], keys, values, allowed)
    return (merged_att, glob_out)

def reference(events, global_tokens, lengths, inner_qkv, inner_out, merge_gain, global_gain, mixed_qkv, mixed_out):
    users, span, width = events.shape
    heads = 16
    head_dim = width // heads
    glob = global_tokens.shape[1]
    merged = lax.map(lambda one: inner_merge(one, inner_qkv, inner_out), events)
    count = merged.shape[1]
    normed = norm_rows(merged, merge_gain)
    gnormed = norm_rows(global_tokens, global_gain)
    qkv = jnp.dot(normed.reshape(users * count, width), mixed_qkv, preferred_element_type=jnp.float32).astype(jnp.bfloat16)
    qkv = qkv.reshape(users, count, 3, heads, head_dim).transpose(0, 3, 1, 2, 4).reshape(users, heads, count, 3 * head_dim)
    gqkv = jnp.dot(gnormed.reshape(users * glob, width), mixed_qkv, preferred_element_type=jnp.float32).astype(jnp.bfloat16)
    gqkv = gqkv.reshape(users, glob, 3, heads, head_dim).transpose(0, 3, 1, 2, 4).reshape(users, heads, glob, 3 * head_dim)
    valid = (lengths // 8).astype(jnp.int32)

    def per_user(item):
        merged_qkv, global_qkv, live = item
        return jax.vmap(lambda a, b: pair_attention(a, b, live))(merged_qkv, global_qkv)
    att_m, att_g = lax.map(per_user, (qkv, gqkv, valid))
    heads_out = att_m.transpose(0, 2, 1, 3).reshape(users * count, width)
    merged_out = merged.astype(jnp.float32).reshape(users * count, width) + jnp.dot(heads_out, mixed_out, preferred_element_type=jnp.float32)
    merged_out = merged_out.astype(jnp.bfloat16).reshape(users, count, width)
    global_heads = att_g.reshape(users * heads // 2, 2, glob * head_dim)
    return (merged_out, global_heads)
```

```python
import functools
import math

import jax
import jax.numpy as jnp
from jax import lax
from jax.experimental import pallas as pl
from jax.experimental.pallas import tpu as pltpu
from jax.sharding import PartitionSpec as P

BF16 = jnp.bfloat16
F32 = jnp.float32
USERS = 16
HEADS = 16
WIDTH = 512
HEAD_DIM = 32
GLOBALS = 128
SPAN = 128
TOKENS = 16
DEVICES = 256
COUNT = DEVICES * TOKENS
STEP_USERS = 4
SCORE_SCALE = math.log2(math.e) / math.sqrt(HEAD_DIM)
SAFE = 100.0
LOW = -1e30


def dot_rows(a, b):
    return lax.dot_general(a, b, (((1,), (0,)), ((), ())), preferred_element_type=F32)


def dot_last(a, b):
    return lax.dot_general(a, b, (((1,), (1,)), ((), ())), preferred_element_type=F32)


def iota(shape, axis):
    return lax.broadcasted_iota(jnp.int32, shape, axis)


def norm_f32(wide, gain):
    scale = lax.rsqrt(jnp.mean(wide * wide, axis=-1, keepdims=True) + 1e-06)
    return wide * scale * gain


def inner_kernel(
    events_ref,
    tokens_ref,
    inner_qkv_ref,
    inner_out_ref,
    merge_gain_ref,
    global_gain_ref,
    mixed_qkv_ref,
    merged_ref,
    payload_ref,
    normed_ref,
):
    step = pl.program_id(0)
    x = events_ref[...].reshape(STEP_USERS * SPAN, WIDTH)
    qkv = dot_rows(x, inner_qkv_ref[...]).astype(BF16)
    lane = iota((SPAN, 128), 1)
    low_half = lane < 64
    lane_group8 = iota((8, 128), 1) // 8
    compact = []
    for b in range(STEP_USERS):
        rows = slice(b * SPAN, (b + 1) * SPAN)
        for t in range(4):
            q = qkv[rows, t * 128 : (t + 1) * 128]
            k = qkv[rows, 512 + t * 128 : 512 + (t + 1) * 128]
            zero = jnp.zeros_like(k)
            both = jnp.concatenate(
                [jnp.where(low_half, k, zero), jnp.where(low_half, zero, k)], axis=0
            )
            scores = dot_last(both, q)
            for half in range(2):
                picked = scores[half * 128 : half * 128 + 8]
                for g in range(1, TOKENS):
                    start = half * 128 + g * 8
                    picked = jnp.where(lane_group8 == g, scores[start : start + 8], picked)
                compact.append(picked)
    sc = jnp.stack(compact, axis=0)
    top = jnp.max(sc, axis=1, keepdims=True)
    expd = jnp.exp((sc - top) * 0.125)
    w = expd / jnp.sum(expd, axis=1, keepdims=True)
    w = w.reshape(STEP_USERS * 64, 128)
    same = (iota((128, 128), 0) // 8 == iota((128, 128), 1) // 8).astype(BF16)
    w_hi = w.astype(BF16)
    w_lo = (w - w_hi.astype(F32)).astype(BF16)
    wm = (dot_rows(w_hi, same) + dot_rows(w_lo, same)) * 0.125
    wm = wm.reshape(STEP_USERS * 8, 8, 128)
    on_diag = iota((8, 128), 0) == iota((8, 128), 1) % 8
    row = jnp.sum(jnp.where(on_diag[None], wm, 0.0), axis=1, keepdims=True)
    group_of_lane = iota((TOKENS, 128), 1) // 8 == iota((TOKENS, 128), 0)
    spread = jnp.where(group_of_lane[None], row, 0.0).astype(BF16)
    mean_w = jnp.where(group_of_lane, 0.125, 0.0).astype(BF16)
    low_half16 = iota((TOKENS, 128), 1) < 64
    pooled, means = [], []
    for b in range(STEP_USERS):
        rows = slice(b * SPAN, (b + 1) * SPAN)
        tiles = []
        for t in range(4):
            a = spread[b * 8 + 2 * t : b * 8 + 2 * t + 2].reshape(2 * TOKENS, 128)
            r = dot_rows(a, qkv[rows, 1024 + t * 128 : 1024 + (t + 1) * 128])
            tiles.append(jnp.where(low_half16, r[:TOKENS], r[TOKENS:]))
        pooled.append(jnp.concatenate(tiles, axis=1))
        means.append(dot_rows(mean_w, x[rows]))
    pooled = jnp.concatenate(pooled, axis=0).astype(BF16)
    merged = jnp.concatenate(means, axis=0) + dot_rows(pooled, inner_out_ref[...])
    merged = merged.astype(BF16)
    merged_ref[...] = merged
    rows = STEP_USERS * TOKENS
    normed = norm_f32(merged.astype(F32), merge_gain_ref[...])
    for c in range(4):
        normed_ref[c, pl.ds(pl.multiple_of(step * rows, rows), rows), :] = normed[
            :, c * 128 : (c + 1) * 128
        ]

    @pl.when(step == USERS // STEP_USERS - 1)
    def _():
        slab_rows = jnp.concatenate(
            [
                jnp.concatenate(
                    [normed_ref[c, pl.ds(i, 2 * USERS, stride=8), :] for i in range(8)], axis=0
                ).astype(BF16)
                for c in range(4)
            ],
            axis=1,
        )
        lane_block = iota((2 * USERS, 128), 1) // HEAD_DIM
        for c in range(3):
            for ht in range(4):
                col = c * 512 + ht * 128
                part = dot_rows(slab_rows, mixed_qkv_ref[:, col : col + 128])
                if c == 0:
                    part = part * SCORE_SCALE
                for t in range(2):
                    base = [
                        part[(t * 4 + j) * 2 * USERS : (t * 4 + j + 1) * 2 * USERS]
                        for j in range(4)
                    ]
                    for hh in range(4):
                        out = None
                        for j in range(4):
                            shift = (HEAD_DIM * (j - hh)) % 128
                            moved = pltpu.roll(base[j], shift, 1) if shift else base[j]
                            out = moved if out is None else jnp.where(lane_block == j, moved, out)
                        tile = (c * 2 + t) * 128
                        payload_ref[:, ht * 4 + hh, :, tile : tile + 128] = out.astype(BF16).reshape(
                            USERS, 2, 128
                        )
        gnormed = norm_f32(tokens_ref[...].astype(F32), global_gain_ref[...]).astype(BF16)
        block16 = iota((USERS, 128), 1) // HEAD_DIM
        for ht in range(4):
            sect = []
            for c in range(3):
                col = c * 512 + ht * 128
                part = dot_rows(gnormed, mixed_qkv_ref[:, col : col + 128])
                sect.append(part * SCORE_SCALE if c == 0 else part)
            for hh in range(4):
                out = jnp.zeros((USERS, 128), F32)
                for c in range(3):
                    shift = (HEAD_DIM * (c - hh)) % 128
                    moved = pltpu.roll(sect[c], shift, 1) if shift else sect[c]
                    out = jnp.where(block16 == c, moved, out)
                payload_ref[:, ht * 4 + hh, :, 768:896] = jnp.broadcast_to(
                    out[:, None, :], (USERS, 2, 128)
                ).astype(BF16)


def inner_call(events, tokens, inner_qkv, inner_out, merge_gain, global_gain, mixed_qkv):
    whole = lambda shape: pl.BlockSpec(shape, lambda i: (0,) * len(shape))
    return pl.pallas_call(
        inner_kernel,
        grid=(USERS // STEP_USERS,),
        in_specs=[
            pl.BlockSpec((STEP_USERS, SPAN, WIDTH), lambda i: (i, 0, 0)),
            whole((USERS, WIDTH)),
            whole((WIDTH, 3 * WIDTH)),
            whole((WIDTH, WIDTH)),
            whole((1, WIDTH)),
            whole((1, WIDTH)),
            whole((WIDTH, 3 * WIDTH)),
        ],
        out_specs=[
            pl.BlockSpec((STEP_USERS * TOKENS, WIDTH), lambda i: (i, 0)),
            whole((USERS, HEADS, 2, 896)),
        ],
        out_shape=[
            jax.ShapeDtypeStruct((USERS * TOKENS, WIDTH), BF16),
            jax.ShapeDtypeStruct((USERS, HEADS, 2, 896), BF16),
        ],
        scratch_shapes=[pltpu.VMEM((4, USERS * TOKENS, 128), F32)],
        compiler_params=pltpu.CompilerParams(
            dimension_semantics=("arbitrary",), vmem_limit_bytes=48 * 2**20
        ),
        name="inner",
    )(events, tokens, inner_qkv, inner_out, merge_gain, global_gain, mixed_qkv)


QT = 512
TILES = COUNT // QT
PR = QT // 8


def attend_kernel(valid_ref, recv_ref, att_ref, glob_ref, q_ref, kt_ref, v_ref, g_ref, acc_ref):
    valid = valid_ref[0]
    lane = iota((512, 128), 1)
    first = lane < HEAD_DIM
    ones = jnp.where(lane == HEAD_DIM, 1.0, 0.0)
    prow = iota((512, 128), 0)
    same = (iota((128, 128), 0) // HEAD_DIM == iota((128, 128), 1) // HEAD_DIM).astype(BF16)

    def tile_of(index):
        return recv_ref[:, :, index * 128 : (index + 1) * 128].reshape(512, 128)

    def top_square(x):
        return jnp.max(dot_rows((x * x).astype(BF16), same))

    g_ref[...] = tile_of(6).astype(F32)
    g = g_ref[pl.ds(0, GLOBALS, stride=4), :]
    g_lane = iota((GLOBALS, 128), 1)
    gq = g.astype(BF16)[:, :HEAD_DIM]
    gkt = g.T.astype(BF16)[HEAD_DIM : 2 * HEAD_DIM]
    gv = jnp.where(g_lane < HEAD_DIM, pltpu.roll(g, 64, 1), jnp.where(g_lane == HEAD_DIM, 1.0, 0.0))
    gv = gv.astype(BF16)
    g_sq = dot_rows((g * g).astype(BF16), same)
    q_top = jnp.max(jnp.where(g_lane < HEAD_DIM, g_sq, 0.0))
    k_top = jnp.max(jnp.where(g_lane // HEAD_DIM == 1, g_sq, 0.0))

    for t in range(2):
        q = tile_of(t).astype(F32)
        k = tile_of(2 + t).astype(F32)
        v = tile_of(4 + t).astype(F32)
        q_top = jnp.maximum(q_top, top_square(q))
        k_top = jnp.maximum(k_top, top_square(k))
        k_t = k.T.astype(BF16)
        for j in range(4):
            i = t * 4 + j
            qi = (pltpu.roll(q, 128 - 32 * j, 1) if j else q).astype(BF16)
            vi = pltpu.roll(v, 128 - 32 * j, 1) if j else v
            vi = jnp.where(prow * 8 + i < valid, jnp.where(first, vi, ones), 0.0).astype(BF16)
            ki = k_t[j * HEAD_DIM : (j + 1) * HEAD_DIM]
            for n in range(TILES):
                at = n * QT + i * PR
                q_ref[at : at + PR, :] = qi[n * PR : (n + 1) * PR]
                v_ref[at : at + PR, :] = vi[n * PR : (n + 1) * PR]
                kt_ref[n, :, i * PR : (i + 1) * PR] = ki[:, n * PR : (n + 1) * PR]

    def place(index):
        return (index % PR) * 8 + index // PR

    out_lane = iota((PR, 128), 1) // HEAD_DIM

    def finish(n, acc):
        o = acc / acc[:, HEAD_DIM : HEAD_DIM + 1]
        for t in range(2):
            packed = o[t * 4 * PR : (t * 4 + 1) * PR]
            for j in range(1, 4):
                i = t * 4 + j
                packed = jnp.where(
                    out_lane == j, pltpu.roll(o[i * PR : (i + 1) * PR], 32 * j, 1), packed
                )
            att_ref[pl.ds(n * (PR // 2), PR // 2), :, t * 128 : (t + 1) * 128] = packed.astype(
                BF16
            ).reshape(PR // 2, 2, 128)

    safe = q_top * k_top * 1.05 < SAFE * SAFE

    @pl.when(safe)
    def _():
        causal = place(iota((QT, QT), 0)) >= place(iota((QT, QT), 1))
        for n in range(TILES):
            q = q_ref[n * QT : (n + 1) * QT, :HEAD_DIM]
            p = jnp.exp2(dot_rows(q, gkt)).astype(BF16)
            acc_ref[...] = dot_rows(p, gv)

            def body(m, carry, q=q):
                s = dot_rows(q, kt_ref[m])
                p = jnp.exp2(s).astype(BF16)
                at = pl.multiple_of(m * QT, QT)
                acc_ref[...] += dot_rows(p, v_ref[pl.ds(at, QT), :])
                return carry

            lax.fori_loop(0, n, body, 0)
            s = dot_rows(q, kt_ref[n])
            p = jnp.where(causal, jnp.exp2(s), 0.0).astype(BF16)
            finish(n, acc_ref[...] + dot_rows(p, v_ref[n * QT : (n + 1) * QT, :]))
        p = jnp.exp2(dot_rows(gq, gkt)).astype(BF16)

        def gbody(m, acc):
            p = jnp.exp2(dot_rows(gq, kt_ref[m])).astype(BF16)
            at = pl.multiple_of(m * QT, QT)
            return acc + dot_rows(p, v_ref[pl.ds(at, QT), :])

        acc = lax.fori_loop(0, TILES, gbody, dot_rows(p, gv))
        o = acc / acc[:, HEAD_DIM : HEAD_DIM + 1]
        glob_ref[...] = o[:, :HEAD_DIM].astype(BF16)

    @pl.when(jnp.logical_not(safe))
    def _():
        def shifted(s, allowed, vals, state):
            top, acc = state
            if allowed is not None:
                s = jnp.where(allowed, s, LOW)
            new = jnp.maximum(top, jnp.max(s, axis=1, keepdims=True))
            p = jnp.exp2(s - new).astype(BF16)
            return new, acc * jnp.exp2(top - new) + dot_rows(p, vals)

        def start(q):
            rows = q.shape[0]
            state = (jnp.full((rows, 1), LOW, F32), jnp.zeros((rows, 128), F32))
            return shifted(dot_rows(q, gkt), None, gv, state)

        def tile(n, carry):
            q = q_ref[pl.ds(pl.multiple_of(n * QT, QT), QT), :][:, :HEAD_DIM]

            def body(m, state):
                row = n * QT + place(iota((QT, QT), 0))
                column = m * QT + place(iota((QT, QT), 1))
                allowed = (row >= column) & (column < valid)
                vals = v_ref[pl.ds(pl.multiple_of(m * QT, QT), QT), :]
                return shifted(dot_rows(q, kt_ref[m]), allowed, vals, state)

            finish(n, lax.fori_loop(0, n + 1, body, start(q))[1])
            return carry

        lax.fori_loop(0, TILES, tile, 0)

        def gbody(m, state):
            allowed = m * QT + place(iota((GLOBALS, QT), 1)) < valid
            vals = v_ref[pl.ds(pl.multiple_of(m * QT, QT), QT), :]
            return shifted(dot_rows(gq, kt_ref[m]), allowed, vals, state)

        acc = lax.fori_loop(0, TILES, gbody, start(gq))[1]
        o = acc / acc[:, HEAD_DIM : HEAD_DIM + 1]
        glob_ref[...] = o[:, :HEAD_DIM].astype(BF16)


def attend_call(valid, recv):
    vmem = pl.BlockSpec(memory_space=pltpu.VMEM)
    return pl.pallas_call(
        attend_kernel,
        in_specs=[pl.BlockSpec(memory_space=pltpu.SMEM), vmem],
        out_specs=[vmem, vmem],
        out_shape=[
            jax.ShapeDtypeStruct((DEVICES, 2, 256), BF16),
            jax.ShapeDtypeStruct((GLOBALS, HEAD_DIM), BF16),
        ],
        scratch_shapes=[
            pltpu.VMEM((COUNT, 128), BF16),
            pltpu.VMEM((TILES, HEAD_DIM, QT), BF16),
            pltpu.VMEM((COUNT, 128), BF16),
            pltpu.VMEM((512, 128), F32),
            pltpu.VMEM((QT, 128), F32),
        ],
        compiler_params=pltpu.CompilerParams(vmem_limit_bytes=48 * 2**20),
        name="attend",
    )(valid, recv)


def output_kernel(back_ref, merged_ref, mixed_out_ref, out_ref, wide_ref, sum_ref):
    for h in range(HEADS):
        rows = mixed_out_ref[h * HEAD_DIM : (h + 1) * HEAD_DIM, :]
        for j in range(4):
            wide_ref[h * 128 + j * HEAD_DIM : h * 128 + (j + 1) * HEAD_DIM, :] = rows
    block = iota((2 * USERS, 128), 1) // HEAD_DIM
    keep = [(block == j).astype(F32).astype(BF16) for j in range(4)]
    parts = [[] for _ in range(8)]
    for h in range(HEADS):
        for t in range(2):
            x = back_ref[:, h, :, t * 128 : (t + 1) * 128].reshape(2 * USERS, 128)
            for j in range(4):
                parts[t * 4 + j].append(x * keep[j])
    lhs = jnp.concatenate([jnp.concatenate(p, axis=1) for p in parts], axis=0)
    prod = dot_rows(lhs, wide_ref[...])
    for c in range(4):
        cols = slice(c * 128, (c + 1) * 128)
        for i in range(8):
            rows = slice(i * 2 * USERS, (i + 1) * 2 * USERS)
            sum_ref[c, pl.ds(i, 2 * USERS, stride=8), :] = prod[rows, cols]
        out_ref[:, cols] = (merged_ref[:, cols].astype(F32) + sum_ref[c]).astype(BF16)


def output_call(back, merged, mixed_out):
    vmem = pl.BlockSpec(memory_space=pltpu.VMEM)
    return pl.pallas_call(
        output_kernel,
        in_specs=[vmem] * 3,
        out_specs=vmem,
        out_shape=jax.ShapeDtypeStruct((USERS * TOKENS, WIDTH), BF16),
        scratch_shapes=[
            pltpu.VMEM((HEADS * 128, WIDTH), BF16),
            pltpu.VMEM((4, USERS * TOKENS, 128), F32),
        ],
        compiler_params=pltpu.CompilerParams(vmem_limit_bytes=48 * 2**20),
        name="output",
    )(back, merged, mixed_out)


def per_device(
    events,
    global_tokens,
    lengths,
    inner_qkv,
    inner_out,
    merge_gain,
    global_gain,
    mixed_qkv,
    mixed_out,
):
    merged, payload = inner_call(
        events,
        global_tokens.reshape(USERS, WIDTH),
        inner_qkv,
        inner_out,
        merge_gain.reshape(1, WIDTH),
        global_gain.reshape(1, WIDTH),
        mixed_qkv,
    )
    arrived = lax.all_to_all(
        payload.reshape(DEVICES, 2, 896), ("seq", "head"), split_axis=0, concat_axis=0, tiled=True
    )
    user = lax.axis_index("seq") // 8
    valid = lax.dynamic_slice_in_dim(lengths, user, 1) // 8
    att, glob = attend_call(valid, arrived)
    back = lax.all_to_all(att, ("seq", "head"), split_axis=0, concat_axis=0, tiled=True)
    out = output_call(back.reshape(USERS, HEADS, 2, 256), merged, mixed_out)
    return (out.reshape(USERS, TOKENS, WIDTH), glob.reshape(1, 1, GLOBALS * HEAD_DIM))


def solution(mesh):
    in_specs = (
        P(None, ("seq", "head"), None),
        P(None, "seq", None),
        P(),
        P(),
        P(),
        P(),
        P(),
        P(),
        P(),
    )
    out_specs = (P(None, ("seq", "head"), None), P("seq", "head", None))
    return jax.shard_map(
        per_device, mesh=mesh, in_specs=in_specs, out_specs=out_specs, check_vma=False
    )
```

```python
import functools
import math

import jax
import jax.numpy as jnp
from jax import lax
from jax.experimental import pallas as pl
from jax.experimental.pallas import tpu as pltpu
from jax.sharding import PartitionSpec as P

BF16 = jnp.bfloat16
F32 = jnp.float32
USERS = 16
HEADS = 16
WIDTH = 512
HEAD_DIM = 32
GLOBALS = 128
SPAN = 128
TOKENS = 16
DEVICES = 256
COUNT = DEVICES * TOKENS
STEP_USERS = 4
SCORE_SCALE = math.log2(math.e) / math.sqrt(HEAD_DIM)
SAFE = 100.0
LOW = -1e30


def dot_rows(a, b):
    return lax.dot_general(a, b, (((1,), (0,)), ((), ())), preferred_element_type=F32)


def dot_last(a, b):
    return lax.dot_general(a, b, (((1,), (1,)), ((), ())), preferred_element_type=F32)


def iota(shape, axis):
    return lax.broadcasted_iota(jnp.int32, shape, axis)


def norm_f32(wide, gain):
    scale = lax.rsqrt(jnp.mean(wide * wide, axis=-1, keepdims=True) + 1e-06)
    return wide * scale * gain


def inner_kernel(
    events_ref,
    tokens_hbm,
    inner_qkv_hbm,
    inner_out_hbm,
    merge_gain_hbm,
    global_gain_hbm,
    mixed_qkv_hbm,
    merged_ref,
    payload_ref,
    normed_ref,
    tokens_ref,
    inner_qkv_ref,
    inner_out_ref,
    merge_gain_ref,
    global_gain_ref,
    mixed_qkv_ref,
    sems,
):
    step = pl.program_id(0)
    fetch = []
    for c in range(3):
        cols = slice(c * WIDTH, (c + 1) * WIDTH)
        fetch.append((inner_qkv_hbm.at[:, cols], inner_qkv_ref.at[:, cols]))
    fetch.append((inner_out_hbm, inner_out_ref))
    fetch.append((merge_gain_hbm, merge_gain_ref))
    for c in range(3):
        cols = slice(c * WIDTH, (c + 1) * WIDTH)
        fetch.append((mixed_qkv_hbm.at[:, cols], mixed_qkv_ref.at[:, cols]))
    fetch.append((tokens_hbm, tokens_ref))
    fetch.append((global_gain_hbm, global_gain_ref))
    copies = [
        pltpu.make_async_copy(src, dst, sems.at[n]) for n, (src, dst) in enumerate(fetch)
    ]

    @pl.when(step == 0)
    def _():
        for copy in copies:
            copy.start()
        for copy in copies[:3]:
            copy.wait()

    x = events_ref[...].reshape(STEP_USERS * SPAN, WIDTH)
    qkv = dot_rows(x, inner_qkv_ref[...]).astype(BF16)
    lane = iota((SPAN, 128), 1)
    low = (lane < 64).astype(F32).astype(BF16)
    high = (lane >= 64).astype(F32).astype(BF16)
    lane_group8 = iota((8, 128), 1) // 8
    compact = []
    for b in range(STEP_USERS):
        rows = slice(b * SPAN, (b + 1) * SPAN)
        for t in range(4):
            q = qkv[rows, t * 128 : (t + 1) * 128]
            k = qkv[rows, 512 + t * 128 : 512 + (t + 1) * 128]
            scores = dot_last(k, jnp.concatenate([q * low, q * high], axis=0))
            for half in range(2):
                part = scores[:, half * 128 : (half + 1) * 128]
                picked = part[0:8]
                for g in range(1, TOKENS):
                    picked = jnp.where(lane_group8 == g, part[g * 8 : g * 8 + 8], picked)
                compact.append(picked)
    sc = jnp.stack(compact, axis=0)
    top = jnp.max(sc, axis=1, keepdims=True)
    expd = jnp.exp((sc - top) * 0.125)
    w = expd / jnp.sum(expd, axis=1, keepdims=True)
    w = w.reshape(STEP_USERS * 64, 128)
    same = (iota((128, 128), 0) // 8 == iota((128, 128), 1) // 8).astype(BF16)
    w_hi = w.astype(BF16)
    w_lo = (w - w_hi.astype(F32)).astype(BF16)
    wm = (dot_rows(w_hi, same) + dot_rows(w_lo, same)) * 0.125
    wm = wm.reshape(STEP_USERS * 8, 8, 128)
    on_diag = iota((8, 128), 0) == iota((8, 128), 1) % 8
    row = jnp.sum(jnp.where(on_diag[None], wm, 0.0), axis=1, keepdims=True)
    group_of_lane = iota((TOKENS, 128), 1) // 8 == iota((TOKENS, 128), 0)
    spread = jnp.where(group_of_lane[None], row, 0.0).astype(BF16)
    mean_w = jnp.where(group_of_lane, 0.125, 0.0).astype(BF16)
    low_half = iota((TOKENS, 128), 1) < 64
    pooled, means = [], []
    for b in range(STEP_USERS):
        rows = slice(b * SPAN, (b + 1) * SPAN)
        tiles = []
        for tp in range(2):
            a = spread[b * 8 + 4 * tp : b * 8 + 4 * tp + 4].reshape(4 * TOKENS, 128)
            r = dot_rows(a, qkv[rows, 1024 + tp * 256 : 1024 + (tp + 1) * 256])
            for t in range(2):
                cols = slice(t * 128, (t + 1) * 128)
                at = 2 * t * TOKENS
                tiles.append(
                    jnp.where(low_half, r[at : at + TOKENS, cols], r[at + TOKENS : at + 2 * TOKENS, cols])
                )
        pooled.append(jnp.concatenate(tiles, axis=1))
        means.append(dot_rows(mean_w, x[rows]))
    pooled = jnp.concatenate(pooled, axis=0).astype(BF16)

    @pl.when(step == 0)
    def _():
        for copy in copies[3:5]:
            copy.wait()

    merged = jnp.concatenate(means, axis=0) + dot_rows(pooled, inner_out_ref[...])
    merged = merged.astype(BF16)
    merged_ref[...] = merged
    rows = STEP_USERS * TOKENS
    normed = norm_f32(merged.astype(F32), merge_gain_ref[...])
    for c in range(4):
        normed_ref[c, pl.ds(pl.multiple_of(step * rows, rows), rows), :] = normed[
            :, c * 128 : (c + 1) * 128
        ]

    @pl.when(step == USERS // STEP_USERS - 1)
    def _():
        for copy in copies[5:]:
            copy.wait()
        slab_rows = jnp.concatenate(
            [
                jnp.concatenate(
                    [normed_ref[c, pl.ds(i, 2 * USERS, stride=8), :] for i in range(8)], axis=0
                ).astype(BF16)
                for c in range(4)
            ],
            axis=1,
        )
        lane_block = iota((2 * USERS, 128), 1) // HEAD_DIM
        for c in range(3):
            for hp in range(2):
                col = c * 512 + hp * 256
                pair = dot_rows(slab_rows, mixed_qkv_ref[:, col : col + 256])
                if c == 0:
                    pair = pair * SCORE_SCALE
                for ht in (2 * hp, 2 * hp + 1):
                    part = pair[:, (ht % 2) * 128 : (ht % 2 + 1) * 128]
                    for t in range(2):
                        base = [
                            part[(t * 4 + j) * 2 * USERS : (t * 4 + j + 1) * 2 * USERS]
                            for j in range(4)
                        ]
                        for hh in range(4):
                            out = None
                            for j in range(4):
                                shift = (HEAD_DIM * (j - hh)) % 128
                                moved = pltpu.roll(base[j], shift, 1) if shift else base[j]
                                out = moved if j == 0 else jnp.where(lane_block == j, moved, out)
                            tile = (c * 2 + t) * 128
                            payload_ref[:, ht * 4 + hh, :, tile : tile + 128] = out.astype(
                                BF16
                            ).reshape(USERS, 2, 128)
        gnormed = norm_f32(tokens_ref[...].astype(F32), global_gain_ref[...]).astype(BF16)
        block16 = iota((USERS, 128), 1) // HEAD_DIM
        gqkv = [
            dot_rows(gnormed, mixed_qkv_ref[:, c * 512 : (c + 1) * 512]) for c in range(3)
        ]
        gqkv[0] = gqkv[0] * SCORE_SCALE
        for ht in range(4):
            sect = [part[:, ht * 128 : (ht + 1) * 128] for part in gqkv]
            for hh in range(4):
                out = jnp.zeros((USERS, 128), F32)
                for c in range(3):
                    shift = (HEAD_DIM * (c - hh)) % 128
                    moved = pltpu.roll(sect[c], shift, 1) if shift else sect[c]
                    out = jnp.where(block16 == c, moved, out)
                payload_ref[:, ht * 4 + hh, :, 768:896] = jnp.broadcast_to(
                    out[:, None, :], (USERS, 2, 128)
                ).astype(BF16)


def inner_call(events, tokens, inner_qkv, inner_out, merge_gain, global_gain, mixed_qkv):
    hbm = pl.BlockSpec(memory_space=pl.ANY)
    return pl.pallas_call(
        inner_kernel,
        grid=(USERS // STEP_USERS,),
        in_specs=[pl.BlockSpec((STEP_USERS, SPAN, WIDTH), lambda i: (i, 0, 0))] + [hbm] * 6,
        out_specs=[
            pl.BlockSpec((STEP_USERS * TOKENS, WIDTH), lambda i: (i, 0)),
            pl.BlockSpec((USERS, HEADS, 2, 896), lambda i: (0, 0, 0, 0)),
        ],
        out_shape=[
            jax.ShapeDtypeStruct((USERS * TOKENS, WIDTH), BF16),
            jax.ShapeDtypeStruct((USERS, HEADS, 2, 896), BF16),
        ],
        scratch_shapes=[
            pltpu.VMEM((4, USERS * TOKENS, 128), F32),
            pltpu.VMEM((USERS, WIDTH), BF16),
            pltpu.VMEM((WIDTH, 3 * WIDTH), BF16),
            pltpu.VMEM((WIDTH, WIDTH), BF16),
            pltpu.VMEM((1, WIDTH), F32),
            pltpu.VMEM((1, WIDTH), F32),
            pltpu.VMEM((WIDTH, 3 * WIDTH), BF16),
            pltpu.SemaphoreType.DMA((10,)),
        ],
        compiler_params=pltpu.CompilerParams(
            dimension_semantics=("arbitrary",), vmem_limit_bytes=60 * 2**20
        ),
        name="inner",
    )(events, tokens, inner_qkv, inner_out, merge_gain, global_gain, mixed_qkv)


QT = 512
TILES = COUNT // QT
PR = QT // 8
VROWS = 48
QUERIES = COUNT + GLOBALS


def place(index):
    return (index % PR) * 8 + index // PR


def attend_kernel(lengths_ref, recv_ref, att_ref, glob_ref, qt_ref, k_ref, vt_ref, g_ref, acc_ref):
    valid = lengths_ref[lax.axis_index("seq") // 8] // 8
    prow = iota((HEAD_DIM, 512), 1)
    same = (iota((128, 128), 0) // HEAD_DIM == iota((128, 128), 1) // HEAD_DIM).astype(BF16)

    def tile_of(index):
        return recv_ref[:, :, index * 128 : (index + 1) * 128].reshape(512, 128)

    g_ref[...] = tile_of(6).astype(F32)
    g = g_ref[pl.ds(0, GLOBALS, stride=4), :]
    gt = g.T
    gk = pltpu.roll(g, 128 - HEAD_DIM, 1).astype(BF16)[:, :HEAD_DIM]
    qt_ref[:, COUNT:] = gt[:HEAD_DIM].astype(BF16)
    one_row = jnp.where(iota((VROWS - HEAD_DIM, GLOBALS), 0) == 0, 1.0, 0.0)
    gvt = jnp.concatenate([gt[2 * HEAD_DIM : 3 * HEAD_DIM], one_row], axis=0).astype(BF16)
    tail_row = iota((VROWS - HEAD_DIM, 512), 0) == 0
    gg = g * g
    g_sq = dot_rows(gg.astype(BF16), same)
    g_lane = iota((GLOBALS, 128), 1) // HEAD_DIM
    k_top = jnp.max(jnp.where(g_lane == 1, g_sq, 0.0))

    for t in range(2):
        q_t = tile_of(t).astype(F32).T.astype(BF16)
        v_t = tile_of(4 + t).astype(F32).T
        k = tile_of(2 + t).astype(F32)
        k_top = jnp.maximum(k_top, jnp.max(dot_rows((k * k).astype(BF16), same)))
        for j in range(4):
            i = t * 4 + j
            band = slice(j * HEAD_DIM, (j + 1) * HEAD_DIM)
            live = prow * 8 + i < valid
            vi = jnp.where(live, v_t[band], 0.0)
            tail = jnp.where(tail_row & live[: VROWS - HEAD_DIM], 1.0, 0.0)
            vi = jnp.concatenate([vi, tail], axis=0).astype(BF16)
            ki = (pltpu.roll(k, 128 - j * HEAD_DIM, 1) if j else k).astype(BF16)
            for n in range(TILES):
                at = n * QT + i * PR
                part = slice(n * PR, (n + 1) * PR)
                qt_ref[:, at : at + PR] = q_t[band, part]
                vt_ref[n, :, i * PR : (i + 1) * PR] = vi[:, part]
                k_ref[at : at + PR, :] = ki[part]

    q_all = qt_ref[...].astype(F32)
    q_top = jnp.max(jnp.sum(q_all * q_all, axis=0, keepdims=True))
    safe = q_top * k_top * 1.05 < SAFE * SAFE

    @pl.when(safe)
    def _():
        acc_ref[...] = dot_rows(gvt, jnp.exp2(dot_rows(gk, qt_ref[...])).astype(BF16))
        causal = place(iota((QT, QT), 1)) >= place(iota((QT, QT), 0))
        for m in range(TILES):
            lo, hi = m * QT, (m + 1) * QT
            k = k_ref[lo:hi, :HEAD_DIM]
            p = jnp.where(causal, jnp.exp2(dot_rows(k, qt_ref[:, lo:hi])), 0.0)
            acc_ref[:, lo:hi] += dot_rows(vt_ref[m], p.astype(BF16))
            p = jnp.exp2(dot_rows(k, qt_ref[:, hi:]))
            acc_ref[:, hi:] += dot_rows(vt_ref[m], p.astype(BF16))

    @pl.when(jnp.logical_not(safe))
    def _():
        lane = iota((QT, QUERIES), 1)
        q_at = jnp.where(lane < COUNT, lane // QT * QT + place(lane % QT), COUNT)
        k_at = place(iota((QT, QUERIES), 0))
        s = dot_rows(gk, qt_ref[...])
        top = jnp.max(s, axis=0, keepdims=True)
        acc_ref[...] = dot_rows(gvt, jnp.exp2(s - top).astype(BF16))

        def body(m, top):
            at = pl.multiple_of(m * QT, QT)
            s = dot_rows(k_ref[pl.ds(at, QT), :][:, :HEAD_DIM], qt_ref[...])
            key = k_at + m * QT
            s = jnp.where((key <= q_at) & (key < valid), s, LOW)
            new = jnp.maximum(top, jnp.max(s, axis=0, keepdims=True))
            p = jnp.exp2(s - new).astype(BF16)
            acc_ref[...] = acc_ref[...] * jnp.exp2(top - new) + dot_rows(vt_ref[m], p)
            return new

        lax.fori_loop(0, TILES, body, top)

    acc = acc_ref[...]
    o = acc[:HEAD_DIM] / acc[HEAD_DIM : HEAD_DIM + 1]
    glob_ref[...] = o[:, COUNT:].T.astype(BF16)
    for t in range(2):
        bands = []
        for j in range(4):
            at = (t * 4 + j) * PR
            bands.append(
                jnp.concatenate([o[:, n * QT + at : n * QT + at + PR] for n in range(TILES)], axis=1)
            )
        packed = jnp.concatenate(bands, axis=0).T.astype(BF16)
        att_ref[:, :, t * 128 : (t + 1) * 128] = packed.reshape(DEVICES, 2, 128)


def attend_call(lengths, recv):
    vmem = pl.BlockSpec(memory_space=pltpu.VMEM)
    return pl.pallas_call(
        attend_kernel,
        in_specs=[pl.BlockSpec(memory_space=pltpu.SMEM), vmem],
        out_specs=[vmem, vmem],
        out_shape=[
            jax.ShapeDtypeStruct((DEVICES, 2, 256), BF16),
            jax.ShapeDtypeStruct((GLOBALS, HEAD_DIM), BF16),
        ],
        scratch_shapes=[
            pltpu.VMEM((HEAD_DIM, QUERIES), BF16),
            pltpu.VMEM((COUNT, 128), BF16),
            pltpu.VMEM((TILES, VROWS, QT), BF16),
            pltpu.VMEM((512, 128), F32),
            pltpu.VMEM((VROWS, QUERIES), F32),
        ],
        compiler_params=pltpu.CompilerParams(vmem_limit_bytes=56 * 2**20),
        name="attend",
    )(lengths, recv)


def output_kernel(back_ref, merged_ref, mixed_out_ref, out_ref, wide_ref, sum_ref):
    for h in range(HEADS):
        rows = mixed_out_ref[h * HEAD_DIM : (h + 1) * HEAD_DIM, :]
        for j in range(4):
            wide_ref[h * 128 + j * HEAD_DIM : h * 128 + (j + 1) * HEAD_DIM, :] = rows
    block = iota((2 * USERS, 128), 1) // HEAD_DIM
    keep = [(block == j).astype(F32).astype(BF16) for j in range(4)]
    parts = [[] for _ in range(8)]
    for h in range(HEADS):
        for t in range(2):
            x = back_ref[:, h, :, t * 128 : (t + 1) * 128].reshape(2 * USERS, 128)
            for j in range(4):
                parts[t * 4 + j].append(x * keep[j])
    lhs = jnp.concatenate([jnp.concatenate(p, axis=1) for p in parts], axis=0)
    prod = dot_rows(lhs, wide_ref[...])
    for c in range(4):
        cols = slice(c * 128, (c + 1) * 128)
        for i in range(8):
            rows = slice(i * 2 * USERS, (i + 1) * 2 * USERS)
            sum_ref[c, pl.ds(i, 2 * USERS, stride=8), :] = prod[rows, cols]
        out_ref[:, cols] = (merged_ref[:, cols].astype(F32) + sum_ref[c]).astype(BF16)


def output_call(back, merged, mixed_out):
    vmem = pl.BlockSpec(memory_space=pltpu.VMEM)
    return pl.pallas_call(
        output_kernel,
        in_specs=[vmem] * 3,
        out_specs=vmem,
        out_shape=jax.ShapeDtypeStruct((USERS * TOKENS, WIDTH), BF16),
        scratch_shapes=[
            pltpu.VMEM((HEADS * 128, WIDTH), BF16),
            pltpu.VMEM((4, USERS * TOKENS, 128), F32),
        ],
        compiler_params=pltpu.CompilerParams(vmem_limit_bytes=48 * 2**20),
        name="output",
    )(back, merged, mixed_out)


def per_device(
    events,
    global_tokens,
    lengths,
    inner_qkv,
    inner_out,
    merge_gain,
    global_gain,
    mixed_qkv,
    mixed_out,
):
    merged, payload = inner_call(
        events,
        global_tokens.reshape(USERS, WIDTH),
        inner_qkv,
        inner_out,
        merge_gain.reshape(1, WIDTH),
        global_gain.reshape(1, WIDTH),
        mixed_qkv,
    )
    arrived = lax.all_to_all(
        payload.reshape(DEVICES, 2, 896), ("seq", "head"), split_axis=0, concat_axis=0, tiled=True
    )
    att, glob = attend_call(lengths, arrived)
    back = lax.all_to_all(att, ("seq", "head"), split_axis=0, concat_axis=0, tiled=True)
    out = output_call(back.reshape(USERS, HEADS, 2, 256), merged, mixed_out)
    return (out.reshape(USERS, TOKENS, WIDTH), glob.reshape(1, 1, GLOBALS * HEAD_DIM))


def solution(mesh):
    in_specs = (
        P(None, ("seq", "head"), None),
        P(None, "seq", None),
        P(),
        P(),
        P(),
        P(),
        P(),
        P(),
        P(),
    )
    out_specs = (P(None, ("seq", "head"), None), P("seq", "head", None))
    return jax.shard_map(
        per_device, mesh=mesh, in_specs=in_specs, out_specs=out_specs, check_vma=False
    )
```

```python
import functools
import math

import jax
import jax.numpy as jnp
from jax import lax
from jax.experimental import pallas as pl
from jax.experimental.pallas import tpu as pltpu
from jax.sharding import PartitionSpec as P

BF16 = jnp.bfloat16
F32 = jnp.float32
USERS = 16
HEADS = 16
WIDTH = 512
HEAD_DIM = 32
GLOBALS = 128
SPAN = 128
TOKENS = 16
DEVICES = 256
COUNT = DEVICES * TOKENS
STEP_USERS = 8
STEPS = USERS // STEP_USERS
SCORE_SCALE = math.log2(math.e) / math.sqrt(HEAD_DIM)
SAFE = 100.0
LOW = -1e30


def dot_rows(a, b):
    return lax.dot_general(a, b, (((1,), (0,)), ((), ())), preferred_element_type=F32)


def dot_last(a, b):
    return lax.dot_general(a, b, (((1,), (1,)), ((), ())), preferred_element_type=F32)


def iota(shape, axis):
    return lax.broadcasted_iota(jnp.int32, shape, axis)


def norm_f32(wide, gain):
    scale = lax.rsqrt(jnp.mean(wide * wide, axis=-1, keepdims=True) + 1e-06)
    return wide * scale * gain


def inner_kernel(
    events_hbm,
    tokens_hbm,
    inner_qkv_hbm,
    inner_out_hbm,
    merge_gain_hbm,
    global_gain_hbm,
    mixed_qkv_hbm,
    merged_ref,
    payload_ref,
    normed_ref,
    events_ref,
    tokens_ref,
    inner_qkv_ref,
    inner_out_ref,
    merge_gain_ref,
    global_gain_ref,
    mixed_qkv_ref,
    sems,
):
    fetch = [(events_hbm.at[0:STEP_USERS], events_ref.at[0:STEP_USERS])]
    for c in range(3):
        cols = slice(c * WIDTH, (c + 1) * WIDTH)
        fetch.append((inner_qkv_hbm.at[:, cols], inner_qkv_ref.at[:, cols]))
    for n in range(1, STEPS):
        users = slice(n * STEP_USERS, (n + 1) * STEP_USERS)
        fetch.append((events_hbm.at[users], events_ref.at[users]))
    fetch.append((inner_out_hbm, inner_out_ref))
    fetch.append((merge_gain_hbm, merge_gain_ref))
    for c in range(3):
        cols = slice(c * WIDTH, (c + 1) * WIDTH)
        fetch.append((mixed_qkv_hbm.at[:, cols], mixed_qkv_ref.at[:, cols]))
    fetch.append((tokens_hbm, tokens_ref))
    fetch.append((global_gain_hbm, global_gain_ref))
    copies = [
        pltpu.make_async_copy(src, dst, sems.at[n]) for n, (src, dst) in enumerate(fetch)
    ]
    for copy in copies:
        copy.start()

    lane = iota((SPAN, 128), 1)
    low = (lane < 64).astype(F32).astype(BF16)
    high = (lane >= 64).astype(F32).astype(BF16)
    lane_group8 = iota((8, 128), 1) // 8

    def project(step):
        for copy in copies[:4] if step == 0 else copies[3 + step : 4 + step]:
            copy.wait()
        x = events_ref[step * STEP_USERS : (step + 1) * STEP_USERS]
        x = x.reshape(STEP_USERS * SPAN, WIDTH)
        return x, dot_rows(x, inner_qkv_ref[...]).astype(BF16)

    def merge(step, x, qkv):
        compact = []
        for b in range(STEP_USERS):
            rows = slice(b * SPAN, (b + 1) * SPAN)
            for t in range(4):
                q = qkv[rows, t * 128 : (t + 1) * 128]
                k = qkv[rows, 512 + t * 128 : 512 + (t + 1) * 128]
                scores = dot_last(k, jnp.concatenate([q * low, q * high], axis=0))
                for half in range(2):
                    part = scores[:, half * 128 : (half + 1) * 128]
                    picked = part[0:8]
                    for g in range(1, TOKENS):
                        picked = jnp.where(lane_group8 == g, part[g * 8 : g * 8 + 8], picked)
                    compact.append(picked)
        sc = jnp.stack(compact, axis=0)
        top = jnp.max(sc, axis=1, keepdims=True)
        expd = jnp.exp((sc - top) * 0.125)
        w = expd / jnp.sum(expd, axis=1, keepdims=True)
        w = w.reshape(STEP_USERS * 64, 128)
        same = (iota((128, 128), 0) // 8 == iota((128, 128), 1) // 8).astype(BF16)
        w_hi = w.astype(BF16)
        w_lo = (w - w_hi.astype(F32)).astype(BF16)
        wm = (dot_rows(w_hi, same) + dot_rows(w_lo, same)) * 0.125
        wm = wm.reshape(STEP_USERS * 8, 8, 128)
        on_diag = iota((8, 128), 0) == iota((8, 128), 1) % 8
        row = jnp.sum(jnp.where(on_diag[None], wm, 0.0), axis=1, keepdims=True)
        group_of_lane = iota((TOKENS, 128), 1) // 8 == iota((TOKENS, 128), 0)
        spread = jnp.where(group_of_lane[None], row, 0.0).astype(BF16)
        mean_w = jnp.where(group_of_lane, 0.125, 0.0).astype(BF16)
        low_half = iota((TOKENS, 128), 1) < 64
        pooled, means = [], []
        for b in range(STEP_USERS):
            rows = slice(b * SPAN, (b + 1) * SPAN)
            tiles = []
            for tp in range(2):
                a = spread[b * 8 + 4 * tp : b * 8 + 4 * tp + 4].reshape(4 * TOKENS, 128)
                r = dot_rows(a, qkv[rows, 1024 + tp * 256 : 1024 + (tp + 1) * 256])
                for t in range(2):
                    cols = slice(t * 128, (t + 1) * 128)
                    at = 2 * t * TOKENS
                    tiles.append(
                        jnp.where(low_half, r[at : at + TOKENS, cols], r[at + TOKENS : at + 2 * TOKENS, cols])
                    )
            pooled.append(jnp.concatenate(tiles, axis=1))
            means.append(dot_rows(mean_w, x[rows]))
        pooled = jnp.concatenate(pooled, axis=0).astype(BF16)

        if step == 0:
            copies[3 + STEPS].wait()
            copies[4 + STEPS].wait()
        merged = jnp.concatenate(means, axis=0) + dot_rows(pooled, inner_out_ref[...])
        merged = merged.astype(BF16)
        rows = STEP_USERS * TOKENS
        merged_ref[step * rows : (step + 1) * rows, :] = merged
        normed = norm_f32(merged.astype(F32), merge_gain_ref[...])
        for c in range(4):
            normed_ref[c, step * rows : (step + 1) * rows, :] = normed[:, c * 128 : (c + 1) * 128]

    ahead = project(0)
    for step in range(STEPS):
        x, qkv = ahead
        if step + 1 < STEPS:
            ahead = project(step + 1)
        merge(step, x, qkv)

    for copy in copies[5 + STEPS :]:
        copy.wait()
    slab_rows = jnp.concatenate(
        [
            jnp.concatenate(
                [normed_ref[c, pl.ds(i, 2 * USERS, stride=8), :] for i in range(8)], axis=0
            ).astype(BF16)
            for c in range(4)
        ],
        axis=1,
    )
    lane_block = iota((2 * USERS, 128), 1) // HEAD_DIM
    for c in range(3):
        for hp in range(2):
            col = c * 512 + hp * 256
            pair = dot_rows(slab_rows, mixed_qkv_ref[:, col : col + 256])
            if c == 0:
                pair = pair * SCORE_SCALE
            for ht in (2 * hp, 2 * hp + 1):
                part = pair[:, (ht % 2) * 128 : (ht % 2 + 1) * 128]
                for t in range(2):
                    base = [
                        part[(t * 4 + j) * 2 * USERS : (t * 4 + j + 1) * 2 * USERS]
                        for j in range(4)
                    ]
                    for hh in range(4):
                        out = None
                        for j in range(4):
                            shift = (HEAD_DIM * (j - hh)) % 128
                            moved = pltpu.roll(base[j], shift, 1) if shift else base[j]
                            out = moved if j == 0 else jnp.where(lane_block == j, moved, out)
                        tile = (c * 2 + t) * 128
                        payload_ref[:, ht * 4 + hh, :, tile : tile + 128] = out.astype(
                            BF16
                        ).reshape(USERS, 2, 128)
    gnormed = norm_f32(tokens_ref[...].astype(F32), global_gain_ref[...]).astype(BF16)
    block16 = iota((USERS, 128), 1) // HEAD_DIM
    gqkv = [
        dot_rows(gnormed, mixed_qkv_ref[:, c * 512 : (c + 1) * 512]) for c in range(3)
    ]
    gqkv[0] = gqkv[0] * SCORE_SCALE
    for ht in range(4):
        sect = [part[:, ht * 128 : (ht + 1) * 128] for part in gqkv]
        for hh in range(4):
            out = jnp.zeros((USERS, 128), F32)
            for c in range(3):
                shift = (HEAD_DIM * (c - hh)) % 128
                moved = pltpu.roll(sect[c], shift, 1) if shift else sect[c]
                out = jnp.where(block16 == c, moved, out)
            payload_ref[:, ht * 4 + hh, :, 768:896] = jnp.broadcast_to(
                out[:, None, :], (USERS, 2, 128)
            ).astype(BF16)


def inner_call(events, tokens, inner_qkv, inner_out, merge_gain, global_gain, mixed_qkv):
    hbm = pl.BlockSpec(memory_space=pl.ANY)
    vmem = pl.BlockSpec(memory_space=pltpu.VMEM)
    return pl.pallas_call(
        inner_kernel,
        in_specs=[hbm] * 7,
        out_specs=[vmem, vmem],
        out_shape=[
            jax.ShapeDtypeStruct((USERS * TOKENS, WIDTH), BF16),
            jax.ShapeDtypeStruct((USERS, HEADS, 2, 896), BF16),
        ],
        scratch_shapes=[
            pltpu.VMEM((4, USERS * TOKENS, 128), F32),
            pltpu.VMEM((USERS, SPAN, WIDTH), BF16),
            pltpu.VMEM((USERS, WIDTH), BF16),
            pltpu.VMEM((WIDTH, 3 * WIDTH), BF16),
            pltpu.VMEM((WIDTH, WIDTH), BF16),
            pltpu.VMEM((1, WIDTH), F32),
            pltpu.VMEM((1, WIDTH), F32),
            pltpu.VMEM((WIDTH, 3 * WIDTH), BF16),
            pltpu.SemaphoreType.DMA((STEPS + 10,)),
        ],
        compiler_params=pltpu.CompilerParams(vmem_limit_bytes=60 * 2**20),
        name="inner",
    )(events, tokens, inner_qkv, inner_out, merge_gain, global_gain, mixed_qkv)


QT = 512
TILES = COUNT // QT
PR = QT // 8
VROWS = 48
QUERIES = COUNT + GLOBALS


def place(index):
    return (index % PR) * 8 + index // PR


def attend_kernel(lengths_ref, recv_ref, att_ref, glob_ref, qt_ref, k_ref, vt_ref, g_ref, acc_ref):
    valid = lengths_ref[lax.axis_index("seq") // 8] // 8
    prow = iota((HEAD_DIM, 512), 1)
    same = (iota((128, 128), 0) // HEAD_DIM == iota((128, 128), 1) // HEAD_DIM).astype(BF16)

    def tile_of(index):
        return recv_ref[:, :, index * 128 : (index + 1) * 128].reshape(512, 128)

    g_ref[...] = tile_of(6).astype(F32)
    g = g_ref[pl.ds(0, GLOBALS, stride=4), :]
    gt = g.T
    gk = pltpu.roll(g, 128 - HEAD_DIM, 1).astype(BF16)[:, :HEAD_DIM]
    qt_ref[:, COUNT:] = gt[:HEAD_DIM].astype(BF16)
    one_row = jnp.where(iota((VROWS - HEAD_DIM, GLOBALS), 0) == 0, 1.0, 0.0)
    gvt = jnp.concatenate([gt[2 * HEAD_DIM : 3 * HEAD_DIM], one_row], axis=0).astype(BF16)
    tail_row = iota((VROWS - HEAD_DIM, 512), 0) == 0
    gg = g * g
    g_sq = dot_rows(gg.astype(BF16), same)
    g_lane = iota((GLOBALS, 128), 1) // HEAD_DIM
    k_top = jnp.max(jnp.where(g_lane == 1, g_sq, 0.0))

    for t in range(2):
        q_t = tile_of(t).astype(F32).T.astype(BF16)
        v_t = tile_of(4 + t).astype(F32).T
        k = tile_of(2 + t).astype(F32)
        k_top = jnp.maximum(k_top, jnp.max(dot_rows((k * k).astype(BF16), same)))
        for j in range(4):
            i = t * 4 + j
            band = slice(j * HEAD_DIM, (j + 1) * HEAD_DIM)
            live = prow * 8 + i < valid
            vi = jnp.where(live, v_t[band], 0.0)
            tail = jnp.where(tail_row & live[: VROWS - HEAD_DIM], 1.0, 0.0)
            vi = jnp.concatenate([vi, tail], axis=0).astype(BF16)
            ki = (pltpu.roll(k, 128 - j * HEAD_DIM, 1) if j else k).astype(BF16)
            for n in range(TILES):
                at = n * QT + i * PR
                part = slice(n * PR, (n + 1) * PR)
                qt_ref[:, at : at + PR] = q_t[band, part]
                vt_ref[n, :, i * PR : (i + 1) * PR] = vi[:, part]
                k_ref[at : at + PR, :] = ki[part]

    q_all = qt_ref[...].astype(F32)
    q_top = jnp.max(jnp.sum(q_all * q_all, axis=0, keepdims=True))
    safe = q_top * k_top * 1.05 < SAFE * SAFE

    @pl.when(safe)
    def _():
        acc_ref[...] = dot_rows(gvt, jnp.exp2(dot_rows(gk, qt_ref[...])).astype(BF16))
        causal = place(iota((QT, QT), 1)) >= place(iota((QT, QT), 0))
        for m in range(TILES):
            lo, hi = m * QT, (m + 1) * QT
            k = k_ref[lo:hi, :HEAD_DIM]
            p = jnp.where(causal, jnp.exp2(dot_rows(k, qt_ref[:, lo:hi])), 0.0)
            acc_ref[:, lo:hi] += dot_rows(vt_ref[m], p.astype(BF16))
            p = jnp.exp2(dot_rows(k, qt_ref[:, hi:]))
            acc_ref[:, hi:] += dot_rows(vt_ref[m], p.astype(BF16))

    @pl.when(jnp.logical_not(safe))
    def _():
        lane = iota((QT, QUERIES), 1)
        q_at = jnp.where(lane < COUNT, lane // QT * QT + place(lane % QT), COUNT)
        k_at = place(iota((QT, QUERIES), 0))
        s = dot_rows(gk, qt_ref[...])
        top = jnp.max(s, axis=0, keepdims=True)
        acc_ref[...] = dot_rows(gvt, jnp.exp2(s - top).astype(BF16))

        def body(m, top):
            at = pl.multiple_of(m * QT, QT)
            s = dot_rows(k_ref[pl.ds(at, QT), :][:, :HEAD_DIM], qt_ref[...])
            key = k_at + m * QT
            s = jnp.where((key <= q_at) & (key < valid), s, LOW)
            new = jnp.maximum(top, jnp.max(s, axis=0, keepdims=True))
            p = jnp.exp2(s - new).astype(BF16)
            acc_ref[...] = acc_ref[...] * jnp.exp2(top - new) + dot_rows(vt_ref[m], p)
            return new

        lax.fori_loop(0, TILES, body, top)

    acc = acc_ref[...]
    o = acc[:HEAD_DIM] / acc[HEAD_DIM : HEAD_DIM + 1]
    glob_ref[...] = o[:, COUNT:].T.astype(BF16)
    for t in range(2):
        bands = []
        for j in range(4):
            at = (t * 4 + j) * PR
            bands.append(
                jnp.concatenate([o[:, n * QT + at : n * QT + at + PR] for n in range(TILES)], axis=1)
            )
        packed = jnp.concatenate(bands, axis=0).T.astype(BF16)
        att_ref[:, :, t * 128 : (t + 1) * 128] = packed.reshape(DEVICES, 2, 128)


def attend_call(lengths, recv):
    vmem = pl.BlockSpec(memory_space=pltpu.VMEM)
    return pl.pallas_call(
        attend_kernel,
        in_specs=[pl.BlockSpec(memory_space=pltpu.SMEM), vmem],
        out_specs=[vmem, vmem],
        out_shape=[
            jax.ShapeDtypeStruct((DEVICES, 2, 256), BF16),
            jax.ShapeDtypeStruct((GLOBALS, HEAD_DIM), BF16),
        ],
        scratch_shapes=[
            pltpu.VMEM((HEAD_DIM, QUERIES), BF16),
            pltpu.VMEM((COUNT, 128), BF16),
            pltpu.VMEM((TILES, VROWS, QT), BF16),
            pltpu.VMEM((512, 128), F32),
            pltpu.VMEM((VROWS, QUERIES), F32),
        ],
        compiler_params=pltpu.CompilerParams(vmem_limit_bytes=56 * 2**20),
        name="attend",
    )(lengths, recv)


def output_kernel(back_ref, merged_ref, mixed_out_ref, out_ref, wide_ref, sum_ref):
    for h in range(HEADS):
        rows = mixed_out_ref[h * HEAD_DIM : (h + 1) * HEAD_DIM, :]
        for j in range(4):
            wide_ref[h * 128 + j * HEAD_DIM : h * 128 + (j + 1) * HEAD_DIM, :] = rows
    block = iota((2 * USERS, 128), 1) // HEAD_DIM
    keep = [(block == j).astype(F32).astype(BF16) for j in range(4)]
    parts = [[] for _ in range(8)]
    for h in range(HEADS):
        for t in range(2):
            x = back_ref[:, h, :, t * 128 : (t + 1) * 128].reshape(2 * USERS, 128)
            for j in range(4):
                parts[t * 4 + j].append(x * keep[j])
    lhs = jnp.concatenate([jnp.concatenate(p, axis=1) for p in parts], axis=0)
    prod = dot_rows(lhs, wide_ref[...])
    for c in range(4):
        cols = slice(c * 128, (c + 1) * 128)
        for i in range(8):
            rows = slice(i * 2 * USERS, (i + 1) * 2 * USERS)
            sum_ref[c, pl.ds(i, 2 * USERS, stride=8), :] = prod[rows, cols]
        out_ref[:, cols] = (merged_ref[:, cols].astype(F32) + sum_ref[c]).astype(BF16)


def output_call(back, merged, mixed_out):
    vmem = pl.BlockSpec(memory_space=pltpu.VMEM)
    return pl.pallas_call(
        output_kernel,
        in_specs=[vmem] * 3,
        out_specs=vmem,
        out_shape=jax.ShapeDtypeStruct((USERS * TOKENS, WIDTH), BF16),
        scratch_shapes=[
            pltpu.VMEM((HEADS * 128, WIDTH), BF16),
            pltpu.VMEM((4, USERS * TOKENS, 128), F32),
        ],
        compiler_params=pltpu.CompilerParams(vmem_limit_bytes=48 * 2**20),
        name="output",
    )(back, merged, mixed_out)


def per_device(
    events,
    global_tokens,
    lengths,
    inner_qkv,
    inner_out,
    merge_gain,
    global_gain,
    mixed_qkv,
    mixed_out,
):
    merged, payload = inner_call(
        events,
        global_tokens.reshape(USERS, WIDTH),
        inner_qkv,
        inner_out,
        merge_gain.reshape(1, WIDTH),
        global_gain.reshape(1, WIDTH),
        mixed_qkv,
    )
    arrived = lax.all_to_all(
        payload.reshape(DEVICES, 2, 896), ("seq", "head"), split_axis=0, concat_axis=0, tiled=True
    )
    att, glob = attend_call(lengths, arrived)
    back = lax.all_to_all(att, ("seq", "head"), split_axis=0, concat_axis=0, tiled=True)
    out = output_call(back.reshape(USERS, HEADS, 2, 256), merged, mixed_out)
    return (out.reshape(USERS, TOKENS, WIDTH), glob.reshape(1, 1, GLOBALS * HEAD_DIM))


def solution(mesh):
    in_specs = (
        P(None, ("seq", "head"), None),
        P(None, "seq", None),
        P(),
        P(),
        P(),
        P(),
        P(),
        P(),
        P(),
    )
    out_specs = (P(None, ("seq", "head"), None), P("seq", "head", None))
    return jax.shard_map(
        per_device, mesh=mesh, in_specs=in_specs, out_specs=out_specs, check_vma=False
    )
```

```python
import functools
import math

import jax
import jax.numpy as jnp
from jax import lax
from jax.experimental import pallas as pl
from jax.experimental.pallas import tpu as pltpu
from jax.sharding import PartitionSpec as P

BF16 = jnp.bfloat16
F32 = jnp.float32
USERS = 16
HEADS = 16
WIDTH = 512
HEAD_DIM = 32
GLOBALS = 128
SPAN = 128
TOKENS = 16
DEVICES = 256
COUNT = DEVICES * TOKENS
STEP_USERS = 8
STEPS = USERS // STEP_USERS
SCORE_SCALE = math.log2(math.e) / math.sqrt(HEAD_DIM)
SAFE = 100.0
LOW = -1e30


def dot_rows(a, b):
    return lax.dot_general(a, b, (((1,), (0,)), ((), ())), preferred_element_type=F32)


def dot_last(a, b):
    return lax.dot_general(a, b, (((1,), (1,)), ((), ())), preferred_element_type=F32)


def iota(shape, axis):
    return lax.broadcasted_iota(jnp.int32, shape, axis)


def norm_f32(wide, gain):
    scale = lax.rsqrt(jnp.mean(wide * wide, axis=-1, keepdims=True) + 1e-06)
    return wide * scale * gain


def inner_kernel(
    events_hbm,
    tokens_hbm,
    inner_qkv_hbm,
    inner_out_hbm,
    merge_gain_hbm,
    global_gain_hbm,
    mixed_qkv_hbm,
    merged_ref,
    payload_ref,
    normed_ref,
    events_ref,
    tokens_ref,
    inner_qkv_ref,
    inner_out_ref,
    merge_gain_ref,
    global_gain_ref,
    mixed_qkv_ref,
    sems,
):
    fetch = [(events_hbm.at[0:STEP_USERS], events_ref.at[0:STEP_USERS])]
    for c in range(3):
        cols = slice(c * WIDTH, (c + 1) * WIDTH)
        fetch.append((inner_qkv_hbm.at[:, cols], inner_qkv_ref.at[:, cols]))
    for n in range(1, STEPS):
        users = slice(n * STEP_USERS, (n + 1) * STEP_USERS)
        fetch.append((events_hbm.at[users], events_ref.at[users]))
    fetch.append((inner_out_hbm, inner_out_ref))
    fetch.append((merge_gain_hbm, merge_gain_ref))
    for c in range(3):
        cols = slice(c * WIDTH, (c + 1) * WIDTH)
        fetch.append((mixed_qkv_hbm.at[:, cols], mixed_qkv_ref.at[:, cols]))
    fetch.append((tokens_hbm, tokens_ref))
    fetch.append((global_gain_hbm, global_gain_ref))
    copies = [
        pltpu.make_async_copy(src, dst, sems.at[n]) for n, (src, dst) in enumerate(fetch)
    ]
    for copy in copies[:4]:
        copy.start()

    lane = iota((SPAN, 128), 1)
    low = (lane < 64).astype(F32).astype(BF16)
    high = (lane >= 64).astype(F32).astype(BF16)
    lane_group8 = iota((8, 128), 1) // 8

    def project(step):
        for copy in copies[:4] if step == 0 else copies[3 + step : 4 + step]:
            copy.wait()
        if step == 0:
            for copy in copies[4:]:
                copy.start()
        x = events_ref[step * STEP_USERS : (step + 1) * STEP_USERS]
        x = x.reshape(STEP_USERS * SPAN, WIDTH)
        return x, dot_rows(x, inner_qkv_ref[...]).astype(BF16)

    def merge(step, x, qkv):
        compact = []
        for b in range(STEP_USERS):
            rows = slice(b * SPAN, (b + 1) * SPAN)
            for t in range(4):
                q = qkv[rows, t * 128 : (t + 1) * 128]
                k = qkv[rows, 512 + t * 128 : 512 + (t + 1) * 128]
                scores = dot_last(k, jnp.concatenate([q * low, q * high], axis=0))
                for half in range(2):
                    part = scores[:, half * 128 : (half + 1) * 128]
                    picked = part[0:8]
                    for g in range(1, TOKENS):
                        picked = jnp.where(lane_group8 == g, part[g * 8 : g * 8 + 8], picked)
                    compact.append(picked)
        sc = jnp.stack(compact, axis=0)
        top = jnp.max(sc, axis=1, keepdims=True)
        expd = jnp.exp((sc - top) * 0.125)
        w = expd / jnp.sum(expd, axis=1, keepdims=True)
        w = w.reshape(STEP_USERS * 64, 128)
        same = (iota((128, 128), 0) // 8 == iota((128, 128), 1) // 8).astype(BF16)
        w_hi = w.astype(BF16)
        w_lo = (w - w_hi.astype(F32)).astype(BF16)
        wm = (dot_rows(w_hi, same) + dot_rows(w_lo, same)) * 0.125
        wm = wm.reshape(STEP_USERS * 8, 8, 128)
        on_diag = iota((8, 128), 0) == iota((8, 128), 1) % 8
        row = jnp.sum(jnp.where(on_diag[None], wm, 0.0), axis=1, keepdims=True)
        group_of_lane = iota((TOKENS, 128), 1) // 8 == iota((TOKENS, 128), 0)
        spread = jnp.where(group_of_lane[None], row, 0.0).astype(BF16)
        mean_w = jnp.where(group_of_lane, 0.125, 0.0).astype(BF16)
        low_half = iota((TOKENS, 128), 1) < 64
        pooled, means = [], []
        for b in range(STEP_USERS):
            rows = slice(b * SPAN, (b + 1) * SPAN)
            tiles = []
            for tp in range(2):
                a = spread[b * 8 + 4 * tp : b * 8 + 4 * tp + 4].reshape(4 * TOKENS, 128)
                r = dot_rows(a, qkv[rows, 1024 + tp * 256 : 1024 + (tp + 1) * 256])
                for t in range(2):
                    cols = slice(t * 128, (t + 1) * 128)
                    at = 2 * t * TOKENS
                    tiles.append(
                        jnp.where(low_half, r[at : at + TOKENS, cols], r[at + TOKENS : at + 2 * TOKENS, cols])
                    )
            pooled.append(jnp.concatenate(tiles, axis=1))
            means.append(dot_rows(mean_w, x[rows]))
        pooled = jnp.concatenate(pooled, axis=0).astype(BF16)

        if step == 0:
            copies[3 + STEPS].wait()
            copies[4 + STEPS].wait()
        merged = jnp.concatenate(means, axis=0) + dot_rows(pooled, inner_out_ref[...])
        merged = merged.astype(BF16)
        rows = STEP_USERS * TOKENS
        merged_ref[step * rows : (step + 1) * rows, :] = merged
        normed = norm_f32(merged.astype(F32), merge_gain_ref[...])
        for c in range(4):
            normed_ref[c, step * rows : (step + 1) * rows, :] = normed[:, c * 128 : (c + 1) * 128]

    ahead = project(0)
    for step in range(STEPS):
        x, qkv = ahead
        if step + 1 < STEPS:
            ahead = project(step + 1)
        merge(step, x, qkv)

    for copy in copies[5 + STEPS :]:
        copy.wait()
    slab_rows = jnp.concatenate(
        [
            jnp.concatenate(
                [normed_ref[c, pl.ds(i, 2 * USERS, stride=8), :] for i in range(8)], axis=0
            ).astype(BF16)
            for c in range(4)
        ],
        axis=1,
    )
    lane_block = iota((2 * USERS, 128), 1) // HEAD_DIM
    for c in range(3):
        for hp in range(2):
            col = c * 512 + hp * 256
            pair = dot_rows(slab_rows, mixed_qkv_ref[:, col : col + 256])
            if c == 0:
                pair = pair * SCORE_SCALE
            for ht in (2 * hp, 2 * hp + 1):
                part = pair[:, (ht % 2) * 128 : (ht % 2 + 1) * 128]
                for t in range(2):
                    base = [
                        part[(t * 4 + j) * 2 * USERS : (t * 4 + j + 1) * 2 * USERS]
                        for j in range(4)
                    ]
                    for hh in range(4):
                        out = None
                        for j in range(4):
                            shift = (HEAD_DIM * (j - hh)) % 128
                            moved = pltpu.roll(base[j], shift, 1) if shift else base[j]
                            out = moved if j == 0 else jnp.where(lane_block == j, moved, out)
                        tile = (c * 2 + t) * 128
                        payload_ref[:, ht * 4 + hh, :, tile : tile + 128] = out.astype(
                            BF16
                        ).reshape(USERS, 2, 128)
    gnormed = norm_f32(tokens_ref[...].astype(F32), global_gain_ref[...]).astype(BF16)
    block16 = iota((USERS, 128), 1) // HEAD_DIM
    gqkv = [
        dot_rows(gnormed, mixed_qkv_ref[:, c * 512 : (c + 1) * 512]) for c in range(3)
    ]
    gqkv[0] = gqkv[0] * SCORE_SCALE
    for ht in range(4):
        sect = [part[:, ht * 128 : (ht + 1) * 128] for part in gqkv]
        for hh in range(4):
            out = jnp.zeros((USERS, 128), F32)
            for c in range(3):
                shift = (HEAD_DIM * (c - hh)) % 128
                moved = pltpu.roll(sect[c], shift, 1) if shift else sect[c]
                out = jnp.where(block16 == c, moved, out)
            payload_ref[:, ht * 4 + hh, :, 768:896] = jnp.broadcast_to(
                out[:, None, :], (USERS, 2, 128)
            ).astype(BF16)


def inner_call(events, tokens, inner_qkv, inner_out, merge_gain, global_gain, mixed_qkv):
    hbm = pl.BlockSpec(memory_space=pl.ANY)
    vmem = pl.BlockSpec(memory_space=pltpu.VMEM)
    return pl.pallas_call(
        inner_kernel,
        in_specs=[hbm] * 7,
        out_specs=[vmem, vmem],
        out_shape=[
            jax.ShapeDtypeStruct((USERS * TOKENS, WIDTH), BF16),
            jax.ShapeDtypeStruct((USERS, HEADS, 2, 896), BF16),
        ],
        scratch_shapes=[
            pltpu.VMEM((4, USERS * TOKENS, 128), F32),
            pltpu.VMEM((USERS, SPAN, WIDTH), BF16),
            pltpu.VMEM((USERS, WIDTH), BF16),
            pltpu.VMEM((WIDTH, 3 * WIDTH), BF16),
            pltpu.VMEM((WIDTH, WIDTH), BF16),
            pltpu.VMEM((1, WIDTH), F32),
            pltpu.VMEM((1, WIDTH), F32),
            pltpu.VMEM((WIDTH, 3 * WIDTH), BF16),
            pltpu.SemaphoreType.DMA((STEPS + 10,)),
        ],
        compiler_params=pltpu.CompilerParams(vmem_limit_bytes=60 * 2**20),
        name="inner",
    )(events, tokens, inner_qkv, inner_out, merge_gain, global_gain, mixed_qkv)


QT = 512
TILES = COUNT // QT
PR = QT // 8
VROWS = 48
QUERIES = COUNT + GLOBALS


def place(index):
    return (index % PR) * 8 + index // PR


def attend_kernel(lengths_ref, recv_ref, att_ref, glob_ref, qt_ref, k_ref, vt_ref, g_ref, acc_ref):
    valid = lengths_ref[lax.axis_index("seq") // 8] // 8
    prow = iota((HEAD_DIM, 512), 1)
    same = (iota((128, 128), 0) // HEAD_DIM == iota((128, 128), 1) // HEAD_DIM).astype(BF16)

    def tile_of(index):
        return recv_ref[:, :, index * 128 : (index + 1) * 128].reshape(512, 128)

    g_ref[...] = tile_of(6).astype(F32)
    g = g_ref[pl.ds(0, GLOBALS, stride=4), :]
    gt = g.T
    gk = pltpu.roll(g, 128 - HEAD_DIM, 1).astype(BF16)[:, :HEAD_DIM]
    qt_ref[:, COUNT:] = gt[:HEAD_DIM].astype(BF16)
    one_row = jnp.where(iota((VROWS - HEAD_DIM, GLOBALS), 0) == 0, 1.0, 0.0)
    gvt = jnp.concatenate([gt[2 * HEAD_DIM : 3 * HEAD_DIM], one_row], axis=0).astype(BF16)
    tail_row = iota((VROWS - HEAD_DIM, 512), 0) == 0
    gg = g * g
    g_sq = dot_rows(gg.astype(BF16), same)
    g_lane = iota((GLOBALS, 128), 1) // HEAD_DIM
    k_top = jnp.max(jnp.where(g_lane == 1, g_sq, 0.0))

    for t in range(2):
        q_t = tile_of(t).astype(F32).T.astype(BF16)
        v_t = tile_of(4 + t).astype(F32).T
        k = tile_of(2 + t).astype(F32)
        k_top = jnp.maximum(k_top, jnp.max(dot_rows((k * k).astype(BF16), same)))
        for j in range(4):
            i = t * 4 + j
            band = slice(j * HEAD_DIM, (j + 1) * HEAD_DIM)
            live = prow * 8 + i < valid
            vi = jnp.where(live, v_t[band], 0.0)
            tail = jnp.where(tail_row & live[: VROWS - HEAD_DIM], 1.0, 0.0)
            vi = jnp.concatenate([vi, tail], axis=0).astype(BF16)
            ki = (pltpu.roll(k, 128 - j * HEAD_DIM, 1) if j else k).astype(BF16)
            for n in range(TILES):
                at = n * QT + i * PR
                part = slice(n * PR, (n + 1) * PR)
                qt_ref[:, at : at + PR] = q_t[band, part]
                vt_ref[n, :, i * PR : (i + 1) * PR] = vi[:, part]
                k_ref[at : at + PR, :] = ki[part]

    q_all = qt_ref[...].astype(F32)
    q_top = jnp.max(jnp.sum(q_all * q_all, axis=0, keepdims=True))
    safe = q_top * k_top * 1.05 < SAFE * SAFE

    @pl.when(safe)
    def _():
        acc_ref[...] = dot_rows(gvt, jnp.exp2(dot_rows(gk, qt_ref[...])).astype(BF16))
        causal = place(iota((QT, QT), 1)) >= place(iota((QT, QT), 0))
        for m in range(TILES):
            lo, hi = m * QT, (m + 1) * QT
            k = k_ref[lo:hi, :HEAD_DIM]
            p = jnp.where(causal, jnp.exp2(dot_rows(k, qt_ref[:, lo:hi])), 0.0)
            acc_ref[:, lo:hi] += dot_rows(vt_ref[m], p.astype(BF16))
            p = jnp.exp2(dot_rows(k, qt_ref[:, hi:]))
            acc_ref[:, hi:] += dot_rows(vt_ref[m], p.astype(BF16))

    @pl.when(jnp.logical_not(safe))
    def _():
        lane = iota((QT, QUERIES), 1)
        q_at = jnp.where(lane < COUNT, lane // QT * QT + place(lane % QT), COUNT)
        k_at = place(iota((QT, QUERIES), 0))
        s = dot_rows(gk, qt_ref[...])
        top = jnp.max(s, axis=0, keepdims=True)
        acc_ref[...] = dot_rows(gvt, jnp.exp2(s - top).astype(BF16))

        def body(m, top):
            at = pl.multiple_of(m * QT, QT)
            s = dot_rows(k_ref[pl.ds(at, QT), :][:, :HEAD_DIM], qt_ref[...])
            key = k_at + m * QT
            s = jnp.where((key <= q_at) & (key < valid), s, LOW)
            new = jnp.maximum(top, jnp.max(s, axis=0, keepdims=True))
            p = jnp.exp2(s - new).astype(BF16)
            acc_ref[...] = acc_ref[...] * jnp.exp2(top - new) + dot_rows(vt_ref[m], p)
            return new

        lax.fori_loop(0, TILES, body, top)

    acc = acc_ref[...]
    o = acc[:HEAD_DIM] / acc[HEAD_DIM : HEAD_DIM + 1]
    glob_ref[...] = o[:, COUNT:].T.astype(BF16)
    for t in range(2):
        bands = []
        for j in range(4):
            at = (t * 4 + j) * PR
            bands.append(
                jnp.concatenate([o[:, n * QT + at : n * QT + at + PR] for n in range(TILES)], axis=1)
            )
        packed = jnp.concatenate(bands, axis=0).T.astype(BF16)
        att_ref[:, :, t * 128 : (t + 1) * 128] = packed.reshape(DEVICES, 2, 128)


def attend_call(lengths, recv):
    vmem = pl.BlockSpec(memory_space=pltpu.VMEM)
    return pl.pallas_call(
        attend_kernel,
        in_specs=[pl.BlockSpec(memory_space=pltpu.SMEM), vmem],
        out_specs=[vmem, vmem],
        out_shape=[
            jax.ShapeDtypeStruct((DEVICES, 2, 256), BF16),
            jax.ShapeDtypeStruct((GLOBALS, HEAD_DIM), BF16),
        ],
        scratch_shapes=[
            pltpu.VMEM((HEAD_DIM, QUERIES), BF16),
            pltpu.VMEM((COUNT, 128), BF16),
            pltpu.VMEM((TILES, VROWS, QT), BF16),
            pltpu.VMEM((512, 128), F32),
            pltpu.VMEM((VROWS, QUERIES), F32),
        ],
        compiler_params=pltpu.CompilerParams(vmem_limit_bytes=32 * 2**20),
        name="attend",
    )(lengths, recv)


def output_kernel(back_ref, merged_ref, mixed_out_ref, out_ref, wide_ref, sum_ref):
    for h in range(HEADS):
        rows = mixed_out_ref[h * HEAD_DIM : (h + 1) * HEAD_DIM, :]
        for j in range(4):
            wide_ref[h * 128 + j * HEAD_DIM : h * 128 + (j + 1) * HEAD_DIM, :] = rows
    block = iota((2 * USERS, 128), 1) // HEAD_DIM
    keep = [(block == j).astype(F32).astype(BF16) for j in range(4)]
    parts = [[] for _ in range(8)]
    for h in range(HEADS):
        for t in range(2):
            x = back_ref[:, h, :, t * 128 : (t + 1) * 128].reshape(2 * USERS, 128)
            for j in range(4):
                parts[t * 4 + j].append(x * keep[j])
    lhs = jnp.concatenate([jnp.concatenate(p, axis=1) for p in parts], axis=0)
    prod = dot_rows(lhs, wide_ref[...])
    for c in range(4):
        cols = slice(c * 128, (c + 1) * 128)
        for i in range(8):
            rows = slice(i * 2 * USERS, (i + 1) * 2 * USERS)
            sum_ref[c, pl.ds(i, 2 * USERS, stride=8), :] = prod[rows, cols]
        out_ref[:, cols] = (merged_ref[:, cols].astype(F32) + sum_ref[c]).astype(BF16)


def output_call(back, merged, mixed_out):
    vmem = pl.BlockSpec(memory_space=pltpu.VMEM)
    return pl.pallas_call(
        output_kernel,
        in_specs=[vmem] * 3,
        out_specs=vmem,
        out_shape=jax.ShapeDtypeStruct((USERS * TOKENS, WIDTH), BF16),
        scratch_shapes=[
            pltpu.VMEM((HEADS * 128, WIDTH), BF16),
            pltpu.VMEM((4, USERS * TOKENS, 128), F32),
        ],
        compiler_params=pltpu.CompilerParams(vmem_limit_bytes=16 * 2**20),
        name="output",
    )(back, merged, mixed_out)


def per_device(
    events,
    global_tokens,
    lengths,
    inner_qkv,
    inner_out,
    merge_gain,
    global_gain,
    mixed_qkv,
    mixed_out,
):
    merged, payload = inner_call(
        events,
        global_tokens.reshape(USERS, WIDTH),
        inner_qkv,
        inner_out,
        merge_gain.reshape(1, WIDTH),
        global_gain.reshape(1, WIDTH),
        mixed_qkv,
    )
    arrived = lax.all_to_all(
        payload.reshape(DEVICES, 2, 896), ("seq", "head"), split_axis=0, concat_axis=0, tiled=True
    )
    att, glob = attend_call(lengths, arrived)
    back = lax.all_to_all(att, ("seq", "head"), split_axis=0, concat_axis=0, tiled=True)
    out = output_call(back.reshape(USERS, HEADS, 2, 256), merged, mixed_out)
    return (out.reshape(USERS, TOKENS, WIDTH), glob.reshape(1, 1, GLOBALS * HEAD_DIM))


def solution(mesh):
    in_specs = (
        P(None, ("seq", "head"), None),
        P(None, "seq", None),
        P(),
        P(),
        P(),
        P(),
        P(),
        P(),
        P(),
    )
    out_specs = (P(None, ("seq", "head"), None), P("seq", "head", None))
    return jax.shard_map(
        per_device, mesh=mesh, in_specs=in_specs, out_specs=out_specs, check_vma=False
    )
```

```python
import functools
import math

import jax
import jax.numpy as jnp
from jax import lax
from jax.experimental import pallas as pl
from jax.experimental.pallas import tpu as pltpu
from jax.sharding import PartitionSpec as P

BF16 = jnp.bfloat16
F32 = jnp.float32
USERS = 16
HEADS = 16
WIDTH = 512
HEAD_DIM = 32
GLOBALS = 128
SPAN = 128
TOKENS = 16
DEVICES = 256
COUNT = DEVICES * TOKENS
STEP_USERS = 8
STEPS = USERS // STEP_USERS
SCORE_SCALE = math.log2(math.e) / math.sqrt(HEAD_DIM)
SAFE = 100.0
LOW = -1e30


def dot_rows(a, b):
    return lax.dot_general(a, b, (((1,), (0,)), ((), ())), preferred_element_type=F32)


def dot_last(a, b):
    return lax.dot_general(a, b, (((1,), (1,)), ((), ())), preferred_element_type=F32)


def iota(shape, axis):
    return lax.broadcasted_iota(jnp.int32, shape, axis)


def norm_f32(wide, gain):
    scale = lax.rsqrt(jnp.mean(wide * wide, axis=-1, keepdims=True) + 1e-06)
    return wide * scale * gain


def inner_kernel(
    events_hbm,
    tokens_hbm,
    inner_qkv_hbm,
    inner_out_hbm,
    merge_gain_hbm,
    global_gain_hbm,
    mixed_qkv_hbm,
    merged_ref,
    payload_ref,
    normed_ref,
    events_ref,
    tokens_ref,
    inner_qkv_ref,
    inner_out_ref,
    merge_gain_ref,
    global_gain_ref,
    mixed_qkv_ref,
    sems,
):
    fetch = [(events_hbm.at[0:STEP_USERS], events_ref.at[0:STEP_USERS])]
    for c in range(3):
        cols = slice(c * WIDTH, (c + 1) * WIDTH)
        fetch.append((inner_qkv_hbm.at[:, cols], inner_qkv_ref.at[:, cols]))
    for n in range(1, STEPS):
        users = slice(n * STEP_USERS, (n + 1) * STEP_USERS)
        fetch.append((events_hbm.at[users], events_ref.at[users]))
    fetch.append((inner_out_hbm, inner_out_ref))
    fetch.append((merge_gain_hbm, merge_gain_ref))
    for c in range(3):
        cols = slice(c * WIDTH, (c + 1) * WIDTH)
        fetch.append((mixed_qkv_hbm.at[:, cols], mixed_qkv_ref.at[:, cols]))
    fetch.append((tokens_hbm, tokens_ref))
    fetch.append((global_gain_hbm, global_gain_ref))
    copies = [
        pltpu.make_async_copy(src, dst, sems.at[n]) for n, (src, dst) in enumerate(fetch)
    ]
    for copy in copies[:4]:
        copy.start()

    lane = iota((SPAN, 128), 1)
    low = (lane < 64).astype(F32).astype(BF16)
    high = (lane >= 64).astype(F32).astype(BF16)
    lane_group8 = iota((8, 128), 1) // 8

    def project(step):
        if step == 0:
            for copy in copies[:4]:
                copy.wait()
            for copy in copies[4:]:
                copy.start()
        x = events_ref[step * STEP_USERS : (step + 1) * STEP_USERS]
        x = x.reshape(STEP_USERS * SPAN, WIDTH)
        return x, dot_rows(x, inner_qkv_ref[...]).astype(BF16)

    def score(qkv):
        compact = []
        for b in range(STEP_USERS):
            rows = slice(b * SPAN, (b + 1) * SPAN)
            for t in range(4):
                q = qkv[rows, t * 128 : (t + 1) * 128]
                k = qkv[rows, 512 + t * 128 : 512 + (t + 1) * 128]
                scores = dot_last(k, jnp.concatenate([q * low, q * high], axis=0))
                for half in range(2):
                    part = scores[:, half * 128 : (half + 1) * 128]
                    picked = part[0:8]
                    for g in range(1, TOKENS):
                        picked = jnp.where(lane_group8 == g, part[g * 8 : g * 8 + 8], picked)
                    compact.append(picked)
        return jnp.stack(compact, axis=0)

    def pool_weights(sc):
        top = jnp.max(sc, axis=1, keepdims=True)
        expd = jnp.exp((sc - top) * 0.125)
        w = expd / jnp.sum(expd, axis=1, keepdims=True)
        w = w.reshape(STEP_USERS * 64, 128)
        same = (iota((128, 128), 0) // 8 == iota((128, 128), 1) // 8).astype(BF16)
        w_hi = w.astype(BF16)
        w_lo = (w - w_hi.astype(F32)).astype(BF16)
        wm = (dot_rows(w_hi, same) + dot_rows(w_lo, same)) * 0.125
        wm = wm.reshape(STEP_USERS * 8, 8, 128)
        on_diag = iota((8, 128), 0) == iota((8, 128), 1) % 8
        row = jnp.sum(jnp.where(on_diag[None], wm, 0.0), axis=1, keepdims=True)
        group_of_lane = iota((TOKENS, 128), 1) // 8 == iota((TOKENS, 128), 0)
        return jnp.where(group_of_lane[None], row, 0.0).astype(BF16)

    def merge(step, x, qkv, spread):
        group_of_lane = iota((TOKENS, 128), 1) // 8 == iota((TOKENS, 128), 0)
        mean_w = jnp.where(group_of_lane, 0.125, 0.0).astype(BF16)
        low_half = iota((TOKENS, 128), 1) < 64
        pooled, means = [], []
        for b in range(STEP_USERS):
            rows = slice(b * SPAN, (b + 1) * SPAN)
            tiles = []
            for tp in range(2):
                a = spread[b * 8 + 4 * tp : b * 8 + 4 * tp + 4].reshape(4 * TOKENS, 128)
                r = dot_rows(a, qkv[rows, 1024 + tp * 256 : 1024 + (tp + 1) * 256])
                for t in range(2):
                    cols = slice(t * 128, (t + 1) * 128)
                    at = 2 * t * TOKENS
                    tiles.append(
                        jnp.where(low_half, r[at : at + TOKENS, cols], r[at + TOKENS : at + 2 * TOKENS, cols])
                    )
            pooled.append(jnp.concatenate(tiles, axis=1))
            means.append(dot_rows(mean_w, x[rows]))
        pooled = jnp.concatenate(pooled, axis=0).astype(BF16)

        merged = jnp.concatenate(means, axis=0) + dot_rows(pooled, inner_out_ref[...])
        merged = merged.astype(BF16)
        rows = STEP_USERS * TOKENS
        merged_ref[step * rows : (step + 1) * rows, :] = merged
        normed = norm_f32(merged.astype(F32), merge_gain_ref[...])
        for c in range(4):
            normed_ref[c, step * rows : (step + 1) * rows, :] = normed[:, c * 128 : (c + 1) * 128]

    held, scores, spreads = {}, {}, {}
    for turn in range(STEPS + 3):
        if turn < STEPS:
            held[turn] = project(turn)
        if 0 <= turn - 1 < STEPS:
            scores[turn - 1] = score(held[turn - 1][1])
        if 0 <= turn - 2 < STEPS:
            spreads[turn - 2] = pool_weights(scores[turn - 2])
        if 0 <= turn - 3 < STEPS:
            merge(turn - 3, *held[turn - 3], spreads[turn - 3])
        if turn == 0:
            for copy in copies[4 : 5 + STEPS]:
                copy.wait()

    for copy in copies[5 + STEPS :]:
        copy.wait()
    slab_rows = jnp.concatenate(
        [
            jnp.concatenate(
                [normed_ref[c, pl.ds(i, 2 * USERS, stride=8), :] for i in range(8)], axis=0
            ).astype(BF16)
            for c in range(4)
        ],
        axis=1,
    )
    lane_block = iota((2 * USERS, 128), 1) // HEAD_DIM
    for c in range(3):
        for hp in range(2):
            col = c * 512 + hp * 256
            pair = dot_rows(slab_rows, mixed_qkv_ref[:, col : col + 256])
            if c == 0:
                pair = pair * SCORE_SCALE
            for ht in (2 * hp, 2 * hp + 1):
                part = pair[:, (ht % 2) * 128 : (ht % 2 + 1) * 128]
                for t in range(2):
                    base = [
                        part[(t * 4 + j) * 2 * USERS : (t * 4 + j + 1) * 2 * USERS]
                        for j in range(4)
                    ]
                    for hh in range(4):
                        out = None
                        for j in range(4):
                            shift = (HEAD_DIM * (j - hh)) % 128
                            moved = pltpu.roll(base[j], shift, 1) if shift else base[j]
                            out = moved if j == 0 else jnp.where(lane_block == j, moved, out)
                        tile = (c * 2 + t) * 128
                        payload_ref[:, ht * 4 + hh, :, tile : tile + 128] = out.astype(
                            BF16
                        ).reshape(USERS, 2, 128)
    gnormed = norm_f32(tokens_ref[...].astype(F32), global_gain_ref[...]).astype(BF16)
    block16 = iota((USERS, 128), 1) // HEAD_DIM
    gqkv = [
        dot_rows(gnormed, mixed_qkv_ref[:, c * 512 : (c + 1) * 512]) for c in range(3)
    ]
    gqkv[0] = gqkv[0] * SCORE_SCALE
    for ht in range(4):
        sect = [part[:, ht * 128 : (ht + 1) * 128] for part in gqkv]
        for hh in range(4):
            out = jnp.zeros((USERS, 128), F32)
            for c in range(3):
                shift = (HEAD_DIM * (c - hh)) % 128
                moved = pltpu.roll(sect[c], shift, 1) if shift else sect[c]
                out = jnp.where(block16 == c, moved, out)
            payload_ref[:, ht * 4 + hh, :, 768:896] = jnp.broadcast_to(
                out[:, None, :], (USERS, 2, 128)
            ).astype(BF16)


def inner_call(events, tokens, inner_qkv, inner_out, merge_gain, global_gain, mixed_qkv):
    hbm = pl.BlockSpec(memory_space=pl.ANY)
    vmem = pl.BlockSpec(memory_space=pltpu.VMEM)
    return pl.pallas_call(
        inner_kernel,
        in_specs=[hbm] * 7,
        out_specs=[vmem, vmem],
        out_shape=[
            jax.ShapeDtypeStruct((USERS * TOKENS, WIDTH), BF16),
            jax.ShapeDtypeStruct((USERS, HEADS, 2, 896), BF16),
        ],
        scratch_shapes=[
            pltpu.VMEM((4, USERS * TOKENS, 128), F32),
            pltpu.VMEM((USERS, SPAN, WIDTH), BF16),
            pltpu.VMEM((USERS, WIDTH), BF16),
            pltpu.VMEM((WIDTH, 3 * WIDTH), BF16),
            pltpu.VMEM((WIDTH, WIDTH), BF16),
            pltpu.VMEM((1, WIDTH), F32),
            pltpu.VMEM((1, WIDTH), F32),
            pltpu.VMEM((WIDTH, 3 * WIDTH), BF16),
            pltpu.SemaphoreType.DMA((STEPS + 10,)),
        ],
        compiler_params=pltpu.CompilerParams(vmem_limit_bytes=60 * 2**20),
        name="inner",
    )(events, tokens, inner_qkv, inner_out, merge_gain, global_gain, mixed_qkv)


QT = 512
TILES = COUNT // QT
PR = QT // 8
VROWS = 48
QUERIES = COUNT + GLOBALS


def place(index):
    return (index % PR) * 8 + index // PR


def attend_kernel(lengths_ref, recv_ref, att_ref, glob_ref, qt_ref, k_ref, vt_ref, g_ref, acc_ref):
    valid = lengths_ref[lax.axis_index("seq") // 8] // 8
    same = (iota((128, 128), 0) // HEAD_DIM == iota((128, 128), 1) // HEAD_DIM).astype(BF16)

    def tile_of(index):
        return recv_ref[:, :, index * 128 : (index + 1) * 128].reshape(512, 128)

    g_ref[...] = tile_of(6).astype(F32)
    g = g_ref[pl.ds(0, GLOBALS, stride=4), :]
    gt = g.T
    gk = pltpu.roll(g, 128 - HEAD_DIM, 1).astype(BF16)[:, :HEAD_DIM]
    qt_ref[:, COUNT:] = gt[:HEAD_DIM].astype(BF16)
    one_row = jnp.where(iota((VROWS - HEAD_DIM, GLOBALS), 0) == 0, 1.0, 0.0)
    gvt = jnp.concatenate([gt[2 * HEAD_DIM : 3 * HEAD_DIM], one_row], axis=0).astype(BF16)
    tail_row = iota((VROWS - HEAD_DIM, 512), 0) == 0
    gg = g * g
    g_sq = dot_rows(gg.astype(BF16), same)
    g_lane = iota((GLOBALS, 128), 1) // HEAD_DIM
    k_top = jnp.max(jnp.where(g_lane == 1, g_sq, 0.0))

    for t in range(2):
        q_t = tile_of(t).astype(F32).T.astype(BF16)
        for j in range(4):
            band = slice(j * HEAD_DIM, (j + 1) * HEAD_DIM)
            for n in range(TILES):
                at = n * QT + (t * 4 + j) * PR
                qt_ref[:, at : at + PR] = q_t[band, n * PR : (n + 1) * PR]

    def finish():
        acc = acc_ref[...]
        o = acc[:HEAD_DIM] / acc[HEAD_DIM : HEAD_DIM + 1]
        glob_ref[...] = o[:, COUNT:].T.astype(BF16)
        for t in range(2):
            bands = []
            for j in range(4):
                at = (t * 4 + j) * PR
                bands.append(
                    jnp.concatenate(
                        [o[:, n * QT + at : n * QT + at + PR] for n in range(TILES)], axis=1
                    )
                )
            packed = jnp.concatenate(bands, axis=0).T.astype(BF16)
            att_ref[:, :, t * 128 : (t + 1) * 128] = packed.reshape(DEVICES, 2, 128)

    acc_ref[...] = dot_rows(gvt, jnp.exp2(dot_rows(gk, qt_ref[...])).astype(BF16))
    causal = place(iota((QT, QT), 1)) >= place(iota((QT, QT), 0))
    v_t = [tile_of(4 + t).astype(F32).T for t in range(2)]
    k_packed = [tile_of(2 + t).astype(F32) for t in range(2)]
    for m in range(TILES):
        lo, hi = m * QT, (m + 1) * QT
        part = slice(m * PR, (m + 1) * PR)
        keys, vals = [], []
        for t in range(2):
            k = k_packed[t][part]
            for j in range(4):
                keys.append(pltpu.roll(k, 128 - j * HEAD_DIM, 1) if j else k)
                vals.append(v_t[t][j * HEAD_DIM : (j + 1) * HEAD_DIM, part])
        k = jnp.concatenate(keys, axis=0).astype(BF16)
        live = place(iota((HEAD_DIM, QT), 1)) + lo < valid
        v = jnp.where(live, jnp.concatenate(vals, axis=1), 0.0)
        tail = jnp.where(tail_row & live[: VROWS - HEAD_DIM], 1.0, 0.0)
        v = jnp.concatenate([v, tail], axis=0).astype(BF16)
        k_ref[lo:hi, :] = k
        vt_ref[m] = v
        k = k[:, :HEAD_DIM]
        p = jnp.where(causal, jnp.exp2(dot_rows(k, qt_ref[:, lo:hi])), 0.0)
        acc_ref[:, lo:hi] += dot_rows(v, p.astype(BF16))
        p = jnp.exp2(dot_rows(k, qt_ref[:, hi:]))
        acc_ref[:, hi:] += dot_rows(v, p.astype(BF16))
    finish()

    q_all = qt_ref[...].astype(F32)
    q_top = jnp.max(jnp.sum(q_all * q_all, axis=0, keepdims=True))
    for t in range(2):
        k = k_packed[t]
        k_top = jnp.maximum(k_top, jnp.max(dot_rows((k * k).astype(BF16), same)))
    safe = q_top * k_top * 1.05 < SAFE * SAFE

    @pl.when(jnp.logical_not(safe))
    def _():
        lane = iota((QT, QUERIES), 1)
        q_at = jnp.where(lane < COUNT, lane // QT * QT + place(lane % QT), COUNT)
        k_at = place(iota((QT, QUERIES), 0))
        s = dot_rows(gk, qt_ref[...])
        top = jnp.max(s, axis=0, keepdims=True)
        acc_ref[...] = dot_rows(gvt, jnp.exp2(s - top).astype(BF16))

        def body(m, top):
            at = pl.multiple_of(m * QT, QT)
            s = dot_rows(k_ref[pl.ds(at, QT), :][:, :HEAD_DIM], qt_ref[...])
            key = k_at + m * QT
            s = jnp.where((key <= q_at) & (key < valid), s, LOW)
            new = jnp.maximum(top, jnp.max(s, axis=0, keepdims=True))
            p = jnp.exp2(s - new).astype(BF16)
            acc_ref[...] = acc_ref[...] * jnp.exp2(top - new) + dot_rows(vt_ref[m], p)
            return new

        lax.fori_loop(0, TILES, body, top)
        finish()


def attend_call(lengths, recv):
    vmem = pl.BlockSpec(memory_space=pltpu.VMEM)
    return pl.pallas_call(
        attend_kernel,
        in_specs=[pl.BlockSpec(memory_space=pltpu.SMEM), vmem],
        out_specs=[vmem, vmem],
        out_shape=[
            jax.ShapeDtypeStruct((DEVICES, 2, 256), BF16),
            jax.ShapeDtypeStruct((GLOBALS, HEAD_DIM), BF16),
        ],
        scratch_shapes=[
            pltpu.VMEM((HEAD_DIM, QUERIES), BF16),
            pltpu.VMEM((COUNT, 128), BF16),
            pltpu.VMEM((TILES, VROWS, QT), BF16),
            pltpu.VMEM((512, 128), F32),
            pltpu.VMEM((VROWS, QUERIES), F32),
        ],
        compiler_params=pltpu.CompilerParams(vmem_limit_bytes=32 * 2**20),
        name="attend",
    )(lengths, recv)


def output_kernel(back_ref, merged_ref, mixed_out_ref, out_ref, wide_ref, sum_ref):
    for h in range(HEADS):
        rows = mixed_out_ref[h * HEAD_DIM : (h + 1) * HEAD_DIM, :]
        for j in range(4):
            wide_ref[h * 128 + j * HEAD_DIM : h * 128 + (j + 1) * HEAD_DIM, :] = rows
    block = iota((2 * USERS, 128), 1) // HEAD_DIM
    keep = [(block == j).astype(F32).astype(BF16) for j in range(4)]
    parts = [[] for _ in range(8)]
    for h in range(HEADS):
        for t in range(2):
            x = back_ref[:, h, :, t * 128 : (t + 1) * 128].reshape(2 * USERS, 128)
            for j in range(4):
                parts[t * 4 + j].append(x * keep[j])
    lhs = jnp.concatenate([jnp.concatenate(p, axis=1) for p in parts], axis=0)
    prod = dot_rows(lhs, wide_ref[...])
    for c in range(4):
        cols = slice(c * 128, (c + 1) * 128)
        for i in range(8):
            rows = slice(i * 2 * USERS, (i + 1) * 2 * USERS)
            sum_ref[c, pl.ds(i, 2 * USERS, stride=8), :] = prod[rows, cols]
        out_ref[:, cols] = (merged_ref[:, cols].astype(F32) + sum_ref[c]).astype(BF16)


def output_call(back, merged, mixed_out):
    vmem = pl.BlockSpec(memory_space=pltpu.VMEM)
    return pl.pallas_call(
        output_kernel,
        in_specs=[vmem] * 3,
        out_specs=vmem,
        out_shape=jax.ShapeDtypeStruct((USERS * TOKENS, WIDTH), BF16),
        scratch_shapes=[
            pltpu.VMEM((HEADS * 128, WIDTH), BF16),
            pltpu.VMEM((4, USERS * TOKENS, 128), F32),
        ],
        compiler_params=pltpu.CompilerParams(vmem_limit_bytes=16 * 2**20),
        name="output",
    )(back, merged, mixed_out)


def per_device(
    events,
    global_tokens,
    lengths,
    inner_qkv,
    inner_out,
    merge_gain,
    global_gain,
    mixed_qkv,
    mixed_out,
):
    merged, payload = inner_call(
        events,
        global_tokens.reshape(USERS, WIDTH),
        inner_qkv,
        inner_out,
        merge_gain.reshape(1, WIDTH),
        global_gain.reshape(1, WIDTH),
        mixed_qkv,
    )
    arrived = lax.all_to_all(
        payload.reshape(DEVICES, 2, 896), ("seq", "head"), split_axis=0, concat_axis=0, tiled=True
    )
    att, glob = attend_call(lengths, arrived)
    back = lax.all_to_all(att, ("seq", "head"), split_axis=0, concat_axis=0, tiled=True)
    out = output_call(back.reshape(USERS, HEADS, 2, 256), merged, mixed_out)
    return (out.reshape(USERS, TOKENS, WIDTH), glob.reshape(1, 1, GLOBALS * HEAD_DIM))


def solution(mesh):
    in_specs = (
        P(None, ("seq", "head"), None),
        P(None, "seq", None),
        P(),
        P(),
        P(),
        P(),
        P(),
        P(),
        P(),
    )
    out_specs = (P(None, ("seq", "head"), None), P("seq", "head", None))
    return jax.shard_map(
        per_device, mesh=mesh, in_specs=in_specs, out_specs=out_specs, check_vma=False
    )
```

```python
import functools
import math

import jax
import jax.numpy as jnp
from jax import lax
from jax.experimental import pallas as pl
from jax.experimental.pallas import tpu as pltpu
from jax.sharding import PartitionSpec as P

BF16 = jnp.bfloat16
F32 = jnp.float32
USERS = 16
HEADS = 16
WIDTH = 512
HEAD_DIM = 32
GLOBALS = 128
SPAN = 128
TOKENS = 16
DEVICES = 256
COUNT = DEVICES * TOKENS
STEP_USERS = 8
STEPS = USERS // STEP_USERS
SCORE_SCALE = math.log2(math.e) / math.sqrt(HEAD_DIM)
SAFE = 100.0
LOW = -1e30


def dot_rows(a, b):
    return lax.dot_general(a, b, (((1,), (0,)), ((), ())), preferred_element_type=F32)


def dot_last(a, b):
    return lax.dot_general(a, b, (((1,), (1,)), ((), ())), preferred_element_type=F32)


def iota(shape, axis):
    return lax.broadcasted_iota(jnp.int32, shape, axis)


def norm_f32(wide, gain):
    scale = lax.rsqrt(jnp.mean(wide * wide, axis=-1, keepdims=True) + 1e-06)
    return wide * scale * gain


def inner_kernel(
    events_hbm,
    tokens_hbm,
    inner_qkv_hbm,
    inner_out_hbm,
    merge_gain_hbm,
    global_gain_hbm,
    mixed_qkv_hbm,
    merged_hbm,
    payload_hbm,
    merged_ref,
    payload_ref,
    normed_ref,
    events_ref,
    tokens_ref,
    inner_qkv_ref,
    inner_out_ref,
    merge_gain_ref,
    global_gain_ref,
    mixed_qkv_ref,
    sems,
):
    fetch = [(events_hbm.at[0:STEP_USERS], events_ref.at[0:STEP_USERS])]
    for c in range(3):
        cols = slice(c * WIDTH, (c + 1) * WIDTH)
        fetch.append((inner_qkv_hbm.at[:, cols], inner_qkv_ref.at[:, cols]))
    for n in range(1, STEPS):
        users = slice(n * STEP_USERS, (n + 1) * STEP_USERS)
        fetch.append((events_hbm.at[users], events_ref.at[users]))
    fetch.append((inner_out_hbm, inner_out_ref))
    fetch.append((merge_gain_hbm, merge_gain_ref))
    for c in range(3):
        cols = slice(c * WIDTH, (c + 1) * WIDTH)
        fetch.append((mixed_qkv_hbm.at[:, cols], mixed_qkv_ref.at[:, cols]))
    fetch.append((tokens_hbm, tokens_ref))
    fetch.append((global_gain_hbm, global_gain_ref))
    copies = [
        pltpu.make_async_copy(src, dst, sems.at[n]) for n, (src, dst) in enumerate(fetch)
    ]
    for copy in copies[:4]:
        copy.start()

    lane = iota((SPAN, 128), 1)
    low = (lane < 64).astype(F32).astype(BF16)
    high = (lane >= 64).astype(F32).astype(BF16)
    lane_group8 = iota((8, 128), 1) // 8

    def project(step):
        if step == 0:
            copies[0].wait()
        x = events_ref[step * STEP_USERS : (step + 1) * STEP_USERS]
        x = x.reshape(STEP_USERS * SPAN, WIDTH)
        if step == 0:
            for copy in copies[1:4]:
                copy.wait()
            for copy in copies[4:]:
                copy.start()
        return x, dot_rows(x, inner_qkv_ref[...]).astype(BF16)

    def score(qkv):
        compact = []
        for b in range(STEP_USERS):
            rows = slice(b * SPAN, (b + 1) * SPAN)
            for t in range(4):
                q = qkv[rows, t * 128 : (t + 1) * 128]
                k = qkv[rows, 512 + t * 128 : 512 + (t + 1) * 128]
                scores = dot_last(k, jnp.concatenate([q * low, q * high], axis=0))
                for half in range(2):
                    part = scores[:, half * 128 : (half + 1) * 128]
                    picked = part[0:8]
                    for g in range(1, TOKENS):
                        picked = jnp.where(lane_group8 == g, part[g * 8 : g * 8 + 8], picked)
                    compact.append(picked)
        return jnp.stack(compact, axis=0)

    def pool_weights(sc):
        top = jnp.max(sc, axis=1, keepdims=True)
        expd = jnp.exp((sc - top) * 0.125)
        w = expd / jnp.sum(expd, axis=1, keepdims=True)
        w = w.reshape(STEP_USERS * 64, 128)
        same = (iota((128, 128), 0) // 8 == iota((128, 128), 1) // 8).astype(BF16)
        w_hi = w.astype(BF16)
        w_lo = (w - w_hi.astype(F32)).astype(BF16)
        wm = (dot_rows(w_hi, same) + dot_rows(w_lo, same)) * 0.125
        wm = wm.reshape(STEP_USERS * 8, 8, 128)
        on_diag = iota((8, 128), 0) == iota((8, 128), 1) % 8
        row = jnp.sum(jnp.where(on_diag[None], wm, 0.0), axis=1, keepdims=True)
        group_of_lane = iota((TOKENS, 128), 1) // 8 == iota((TOKENS, 128), 0)
        return jnp.where(group_of_lane[None], row, 0.0).astype(BF16)

    def merge(step, x, qkv, spread):
        group_of_lane = iota((TOKENS, 128), 1) // 8 == iota((TOKENS, 128), 0)
        mean_w = jnp.where(group_of_lane, 0.125, 0.0).astype(BF16)
        low_half = iota((TOKENS, 128), 1) < 64
        pooled, means = [], []
        for b in range(STEP_USERS):
            rows = slice(b * SPAN, (b + 1) * SPAN)
            tiles = []
            for tp in range(2):
                a = spread[b * 8 + 4 * tp : b * 8 + 4 * tp + 4].reshape(4 * TOKENS, 128)
                r = dot_rows(a, qkv[rows, 1024 + tp * 256 : 1024 + (tp + 1) * 256])
                for t in range(2):
                    cols = slice(t * 128, (t + 1) * 128)
                    at = 2 * t * TOKENS
                    tiles.append(
                        jnp.where(low_half, r[at : at + TOKENS, cols], r[at + TOKENS : at + 2 * TOKENS, cols])
                    )
            pooled.append(jnp.concatenate(tiles, axis=1))
            means.append(dot_rows(mean_w, x[rows]))
        pooled = jnp.concatenate(pooled, axis=0).astype(BF16)

        merged = jnp.concatenate(means, axis=0) + dot_rows(pooled, inner_out_ref[...])
        merged = merged.astype(BF16)
        rows = STEP_USERS * TOKENS
        merged_ref[step * rows : (step + 1) * rows, :] = merged
        normed = norm_f32(merged.astype(F32), merge_gain_ref[...])
        for c in range(4):
            normed_ref[c, step * rows : (step + 1) * rows, :] = normed[:, c * 128 : (c + 1) * 128]

    half = 2 * STEP_USERS
    lane_block = iota((half, 128), 1) // HEAD_DIM

    def pack(step):
        users = slice(step * STEP_USERS, (step + 1) * STEP_USERS)
        first = step * STEP_USERS * TOKENS
        slab_rows = jnp.concatenate(
            [
                jnp.concatenate(
                    [normed_ref[c, pl.ds(first + i, half, stride=8), :] for i in range(8)], axis=0
                ).astype(BF16)
                for c in range(4)
            ],
            axis=1,
        )
        for c in range(3):
            for hp in range(2):
                col = c * 512 + hp * 256
                pair = dot_rows(slab_rows, mixed_qkv_ref[:, col : col + 256])
                if c == 0:
                    pair = pair * SCORE_SCALE
                for ht in (2 * hp, 2 * hp + 1):
                    part = pair[:, (ht % 2) * 128 : (ht % 2 + 1) * 128]
                    for t in range(2):
                        base = [part[(t * 4 + j) * half : (t * 4 + j + 1) * half] for j in range(4)]
                        for hh in range(4):
                            out = None
                            for j in range(4):
                                shift = (HEAD_DIM * (j - hh)) % 128
                                moved = pltpu.roll(base[j], shift, 1) if shift else base[j]
                                out = moved if j == 0 else jnp.where(lane_block == j, moved, out)
                            tile = (c * 2 + t) * 128
                            payload_ref[users, ht * 4 + hh, :, tile : tile + 128] = out.astype(
                                BF16
                            ).reshape(STEP_USERS, 2, 128)

    def pack_globals():
        gnormed = norm_f32(tokens_ref[...].astype(F32), global_gain_ref[...]).astype(BF16)
        block16 = iota((USERS, 128), 1) // HEAD_DIM
        gqkv = [dot_rows(gnormed, mixed_qkv_ref[:, c * 512 : (c + 1) * 512]) for c in range(3)]
        gqkv[0] = gqkv[0] * SCORE_SCALE
        for ht in range(4):
            sect = [part[:, ht * 128 : (ht + 1) * 128] for part in gqkv]
            for hh in range(4):
                out = jnp.zeros((USERS, 128), F32)
                for c in range(3):
                    shift = (HEAD_DIM * (c - hh)) % 128
                    moved = pltpu.roll(sect[c], shift, 1) if shift else sect[c]
                    out = jnp.where(block16 == c, moved, out)
                payload_ref[:, ht * 4 + hh, :, 768:896] = jnp.broadcast_to(
                    out[:, None, :], (USERS, 2, 128)
                ).astype(BF16)

    held, scores, spreads, sent = {}, {}, {}, []
    for turn in range(STEPS + 4):
        if turn < STEPS:
            held[turn] = project(turn)
        if 0 <= turn - 1 < STEPS:
            scores[turn - 1] = score(held[turn - 1][1])
        if 0 <= turn - 2 < STEPS:
            spreads[turn - 2] = pool_weights(scores[turn - 2])
        if 0 <= turn - 3 < STEPS:
            merge(turn - 3, *held[turn - 3], spreads[turn - 3])
        if 0 <= turn - 4 < STEPS:
            pack(turn - 4)
            users = slice((turn - 4) * STEP_USERS, (turn - 3) * STEP_USERS)
            sent.append(
                pltpu.make_async_copy(
                    payload_ref.at[users], payload_hbm.at[users], sems.at[STEPS + 10 + turn - 4]
                )
            )
            sent[-1].start()
        if turn == 0:
            for copy in copies[4:]:
                copy.wait()
        if turn == 1:
            pack_globals()
        if turn == STEPS + 2:
            sent.append(pltpu.make_async_copy(merged_ref, merged_hbm, sems.at[2 * STEPS + 10]))
            sent[-1].start()
    for copy in sent:
        copy.wait()


def inner_call(events, tokens, inner_qkv, inner_out, merge_gain, global_gain, mixed_qkv):
    hbm = pl.BlockSpec(memory_space=pl.ANY)
    return pl.pallas_call(
        inner_kernel,
        in_specs=[hbm] * 7,
        out_specs=[hbm, hbm],
        out_shape=[
            jax.ShapeDtypeStruct((USERS * TOKENS, WIDTH), BF16),
            jax.ShapeDtypeStruct((USERS, HEADS, 2, 896), BF16),
        ],
        scratch_shapes=[
            pltpu.VMEM((USERS * TOKENS, WIDTH), BF16),
            pltpu.VMEM((USERS, HEADS, 2, 896), BF16),
            pltpu.VMEM((4, USERS * TOKENS, 128), F32),
            pltpu.VMEM((USERS, SPAN, WIDTH), BF16),
            pltpu.VMEM((USERS, WIDTH), BF16),
            pltpu.VMEM((WIDTH, 3 * WIDTH), BF16),
            pltpu.VMEM((WIDTH, WIDTH), BF16),
            pltpu.VMEM((1, WIDTH), F32),
            pltpu.VMEM((1, WIDTH), F32),
            pltpu.VMEM((WIDTH, 3 * WIDTH), BF16),
            pltpu.SemaphoreType.DMA((2 * STEPS + 11,)),
        ],
        compiler_params=pltpu.CompilerParams(vmem_limit_bytes=60 * 2**20),
        name="inner",
    )(events, tokens, inner_qkv, inner_out, merge_gain, global_gain, mixed_qkv)


QT = 512
TILES = COUNT // QT
PR = QT // 8
VROWS = 48
QUERIES = COUNT + GLOBALS


def place(index):
    return (index % PR) * 8 + index // PR


def attend_kernel(lengths_ref, recv_ref, att_ref, glob_ref, qt_ref, k_ref, vt_ref, g_ref, acc_ref):
    valid = lengths_ref[lax.axis_index("seq") // 8] // 8
    same = (iota((128, 128), 0) // HEAD_DIM == iota((128, 128), 1) // HEAD_DIM).astype(BF16)

    def tile_of(index):
        return recv_ref[:, :, index * 128 : (index + 1) * 128].reshape(512, 128)

    g_ref[...] = tile_of(6).astype(F32)
    g = g_ref[pl.ds(0, GLOBALS, stride=4), :]
    gt = g.T
    gk = pltpu.roll(g, 128 - HEAD_DIM, 1).astype(BF16)[:, :HEAD_DIM]
    qt_ref[:, COUNT:] = gt[:HEAD_DIM].astype(BF16)
    one_row = jnp.where(iota((VROWS - HEAD_DIM, GLOBALS), 0) == 0, 1.0, 0.0)
    gvt = jnp.concatenate([gt[2 * HEAD_DIM : 3 * HEAD_DIM], one_row], axis=0).astype(BF16)
    tail_row = iota((VROWS - HEAD_DIM, 512), 0) == 0
    gg = g * g
    g_sq = dot_rows(gg.astype(BF16), same)
    g_lane = iota((GLOBALS, 128), 1) // HEAD_DIM
    k_top = jnp.max(jnp.where(g_lane == 1, g_sq, 0.0))

    for t in range(2):
        q_t = tile_of(t).astype(F32).T.astype(BF16)
        for j in range(4):
            band = slice(j * HEAD_DIM, (j + 1) * HEAD_DIM)
            for n in range(TILES):
                at = n * QT + (t * 4 + j) * PR
                qt_ref[:, at : at + PR] = q_t[band, n * PR : (n + 1) * PR]

    def finish():
        acc = acc_ref[...]
        o = acc[:HEAD_DIM] / acc[HEAD_DIM : HEAD_DIM + 1]
        glob_ref[...] = o[:, COUNT:].T.astype(BF16)
        for t in range(2):
            bands = []
            for j in range(4):
                at = (t * 4 + j) * PR
                bands.append(
                    jnp.concatenate(
                        [o[:, n * QT + at : n * QT + at + PR] for n in range(TILES)], axis=1
                    )
                )
            packed = jnp.concatenate(bands, axis=0).T.astype(BF16)
            att_ref[:, :, t * 128 : (t + 1) * 128] = packed.reshape(DEVICES, 2, 128)

    acc_ref[...] = dot_rows(gvt, jnp.exp2(dot_rows(gk, qt_ref[...])).astype(BF16))
    causal = place(iota((QT, QT), 1)) >= place(iota((QT, QT), 0))
    v_t = [tile_of(4 + t).astype(F32).T for t in range(2)]
    k_packed = [tile_of(2 + t).astype(F32) for t in range(2)]
    for m in range(TILES):
        lo, hi = m * QT, (m + 1) * QT
        part = slice(m * PR, (m + 1) * PR)
        keys, vals = [], []
        for t in range(2):
            k = k_packed[t][part]
            for j in range(4):
                keys.append(pltpu.roll(k, 128 - j * HEAD_DIM, 1) if j else k)
                vals.append(v_t[t][j * HEAD_DIM : (j + 1) * HEAD_DIM, part])
        k = jnp.concatenate(keys, axis=0).astype(BF16)
        live = place(iota((HEAD_DIM, QT), 1)) + lo < valid
        v = jnp.where(live, jnp.concatenate(vals, axis=1), 0.0)
        tail = jnp.where(tail_row & live[: VROWS - HEAD_DIM], 1.0, 0.0)
        v = jnp.concatenate([v, tail], axis=0).astype(BF16)
        k_ref[lo:hi, :] = k
        vt_ref[m] = v
        k = k[:, :HEAD_DIM]
        p = jnp.exp2(dot_rows(k, qt_ref[:, lo:]))
        p = jnp.concatenate([jnp.where(causal, p[:, :QT], 0.0), p[:, QT:]], axis=1)
        acc_ref[:, lo:] += dot_rows(v, p.astype(BF16))
    finish()

    q_all = qt_ref[...].astype(F32)
    q_top = jnp.max(jnp.sum(q_all * q_all, axis=0, keepdims=True))
    for t in range(2):
        k = k_packed[t]
        k_top = jnp.maximum(k_top, jnp.max(dot_rows((k * k).astype(BF16), same)))
    safe = q_top * k_top * 1.05 < SAFE * SAFE

    @pl.when(jnp.logical_not(safe))
    def _():
        lane = iota((QT, QUERIES), 1)
        q_at = jnp.where(lane < COUNT, lane // QT * QT + place(lane % QT), COUNT)
        k_at = place(iota((QT, QUERIES), 0))
        s = dot_rows(gk, qt_ref[...])
        top = jnp.max(s, axis=0, keepdims=True)
        acc_ref[...] = dot_rows(gvt, jnp.exp2(s - top).astype(BF16))

        def body(m, top):
            at = pl.multiple_of(m * QT, QT)
            s = dot_rows(k_ref[pl.ds(at, QT), :][:, :HEAD_DIM], qt_ref[...])
            key = k_at + m * QT
            s = jnp.where((key <= q_at) & (key < valid), s, LOW)
            new = jnp.maximum(top, jnp.max(s, axis=0, keepdims=True))
            p = jnp.exp2(s - new).astype(BF16)
            acc_ref[...] = acc_ref[...] * jnp.exp2(top - new) + dot_rows(vt_ref[m], p)
            return new

        lax.fori_loop(0, TILES, body, top)
        finish()


def attend_call(lengths, recv):
    vmem = pl.BlockSpec(memory_space=pltpu.VMEM)
    return pl.pallas_call(
        attend_kernel,
        in_specs=[pl.BlockSpec(memory_space=pltpu.SMEM), vmem],
        out_specs=[vmem, vmem],
        out_shape=[
            jax.ShapeDtypeStruct((DEVICES, 2, 256), BF16),
            jax.ShapeDtypeStruct((GLOBALS, HEAD_DIM), BF16),
        ],
        scratch_shapes=[
            pltpu.VMEM((HEAD_DIM, QUERIES), BF16),
            pltpu.VMEM((COUNT, 128), BF16),
            pltpu.VMEM((TILES, VROWS, QT), BF16),
            pltpu.VMEM((512, 128), F32),
            pltpu.VMEM((VROWS, QUERIES), F32),
        ],
        compiler_params=pltpu.CompilerParams(vmem_limit_bytes=32 * 2**20),
        name="attend",
    )(lengths, recv)


def output_kernel(back_ref, merged_ref, mixed_out_ref, out_ref, wide_ref, sum_ref):
    for h in range(HEADS):
        rows = mixed_out_ref[h * HEAD_DIM : (h + 1) * HEAD_DIM, :]
        for j in range(4):
            wide_ref[h * 128 + j * HEAD_DIM : h * 128 + (j + 1) * HEAD_DIM, :] = rows
    block = iota((2 * USERS, 128), 1) // HEAD_DIM
    keep = [(block == j).astype(F32).astype(BF16) for j in range(4)]
    parts = [[] for _ in range(8)]
    for h in range(HEADS):
        for t in range(2):
            x = back_ref[:, h, :, t * 128 : (t + 1) * 128].reshape(2 * USERS, 128)
            for j in range(4):
                parts[t * 4 + j].append(x * keep[j])
    lhs = jnp.concatenate([jnp.concatenate(p, axis=1) for p in parts], axis=0)
    prod = dot_rows(lhs, wide_ref[...])
    for c in range(4):
        cols = slice(c * 128, (c + 1) * 128)
        for i in range(8):
            rows = slice(i * 2 * USERS, (i + 1) * 2 * USERS)
            sum_ref[c, pl.ds(i, 2 * USERS, stride=8), :] = prod[rows, cols]
        out_ref[:, cols] = (merged_ref[:, cols].astype(F32) + sum_ref[c]).astype(BF16)


def output_call(back, merged, mixed_out):
    vmem = pl.BlockSpec(memory_space=pltpu.VMEM)
    return pl.pallas_call(
        output_kernel,
        in_specs=[vmem] * 3,
        out_specs=vmem,
        out_shape=jax.ShapeDtypeStruct((USERS * TOKENS, WIDTH), BF16),
        scratch_shapes=[
            pltpu.VMEM((HEADS * 128, WIDTH), BF16),
            pltpu.VMEM((4, USERS * TOKENS, 128), F32),
        ],
        compiler_params=pltpu.CompilerParams(vmem_limit_bytes=16 * 2**20),
        name="output",
    )(back, merged, mixed_out)


def per_device(
    events,
    global_tokens,
    lengths,
    inner_qkv,
    inner_out,
    merge_gain,
    global_gain,
    mixed_qkv,
    mixed_out,
):
    merged, payload = inner_call(
        events,
        global_tokens.reshape(USERS, WIDTH),
        inner_qkv,
        inner_out,
        merge_gain.reshape(1, WIDTH),
        global_gain.reshape(1, WIDTH),
        mixed_qkv,
    )
    arrived = lax.all_to_all(
        payload.reshape(DEVICES, 2, 896), ("seq", "head"), split_axis=0, concat_axis=0, tiled=True
    )
    att, glob = attend_call(lengths, arrived)
    back = lax.all_to_all(att, ("seq", "head"), split_axis=0, concat_axis=0, tiled=True)
    out = output_call(back.reshape(USERS, HEADS, 2, 256), merged, mixed_out)
    return (out.reshape(USERS, TOKENS, WIDTH), glob.reshape(1, 1, GLOBALS * HEAD_DIM))


def solution(mesh):
    in_specs = (
        P(None, ("seq", "head"), None),
        P(None, "seq", None),
        P(),
        P(),
        P(),
        P(),
        P(),
        P(),
        P(),
    )
    out_specs = (P(None, ("seq", "head"), None), P("seq", "head", None))
    return jax.shard_map(
        per_device, mesh=mesh, in_specs=in_specs, out_specs=out_specs, check_vma=False
    )
```

```python
import functools
import math

import jax
import jax.numpy as jnp
from jax import lax
from jax.experimental import pallas as pl
from jax.experimental.pallas import tpu as pltpu
from jax.sharding import PartitionSpec as P

BF16 = jnp.bfloat16
F32 = jnp.float32
USERS = 16
HEADS = 16
WIDTH = 512
HEAD_DIM = 32
GLOBALS = 128
SPAN = 128
TOKENS = 16
DEVICES = 256
COUNT = DEVICES * TOKENS
STEP_USERS = 8
STEPS = USERS // STEP_USERS
SCORE_SCALE = math.log2(math.e) / math.sqrt(HEAD_DIM)
SAFE = 100.0
LOW = -1e30
PAD = 8


def dot_rows(a, b):
    return lax.dot_general(a, b, (((1,), (0,)), ((), ())), preferred_element_type=F32)


def dot_last(a, b):
    return lax.dot_general(a, b, (((1,), (1,)), ((), ())), preferred_element_type=F32)


def iota(shape, axis):
    return lax.broadcasted_iota(jnp.int32, shape, axis)


def norm_f32(wide, gain):
    scale = lax.rsqrt(jnp.mean(wide * wide, axis=-1, keepdims=True) + 1e-06)
    return wide * scale * gain


def inner_kernel(
    events_hbm,
    tokens_hbm,
    inner_qkv_hbm,
    inner_out_hbm,
    merge_gain_hbm,
    global_gain_hbm,
    mixed_qkv_hbm,
    merged_hbm,
    payload_hbm,
    merged_ref,
    payload_ref,
    normed_ref,
    events_ref,
    tokens_ref,
    inner_qkv_ref,
    inner_out_ref,
    merge_gain_ref,
    global_gain_ref,
    mixed_qkv_ref,
    sems,
):
    fetch = [(events_hbm.at[0:STEP_USERS], events_ref.at[0:STEP_USERS])]
    for c in range(3):
        cols = slice(c * WIDTH, (c + 1) * WIDTH)
        fetch.append((inner_qkv_hbm.at[:, cols], inner_qkv_ref.at[:, cols]))
    for n in range(1, STEPS):
        users = slice(n * STEP_USERS, (n + 1) * STEP_USERS)
        fetch.append((events_hbm.at[users], events_ref.at[users]))
    fetch.append((inner_out_hbm, inner_out_ref))
    fetch.append((merge_gain_hbm, merge_gain_ref))
    for c in range(3):
        cols = slice(c * WIDTH, (c + 1) * WIDTH)
        fetch.append((mixed_qkv_hbm.at[:, cols], mixed_qkv_ref.at[:, cols]))
    fetch.append((tokens_hbm, tokens_ref))
    fetch.append((global_gain_hbm, global_gain_ref))
    copies = [
        pltpu.make_async_copy(src, dst, sems.at[n]) for n, (src, dst) in enumerate(fetch)
    ]
    for copy in copies[:4]:
        copy.start()

    lane = iota((SPAN, 128), 1)
    low = (lane < 64).astype(F32).astype(BF16)
    high = (lane >= 64).astype(F32).astype(BF16)
    lane_group8 = iota((8, 128), 1) // 8

    def project(step):
        if step == 0:
            copies[0].wait()
        x = events_ref[step * STEP_USERS : (step + 1) * STEP_USERS]
        x = x.reshape(STEP_USERS * SPAN, WIDTH)
        if step == 0:
            for copy in copies[1:4]:
                copy.wait()
            for copy in copies[4:]:
                copy.start()
        return x, dot_rows(x, inner_qkv_ref[...]).astype(BF16)

    def score(qkv):
        compact = []
        for b in range(STEP_USERS):
            rows = slice(b * SPAN, (b + 1) * SPAN)
            for t in range(4):
                q = qkv[rows, t * 128 : (t + 1) * 128]
                k = qkv[rows, 512 + t * 128 : 512 + (t + 1) * 128]
                scores = dot_last(k, jnp.concatenate([q * low, q * high], axis=0))
                for half in range(2):
                    part = scores[:, half * 128 : (half + 1) * 128]
                    picked = part[0:8]
                    for g in range(1, TOKENS):
                        picked = jnp.where(lane_group8 == g, part[g * 8 : g * 8 + 8], picked)
                    compact.append(picked)
        return jnp.stack(compact, axis=0)

    def pool_weights(sc):
        top = jnp.max(sc, axis=1, keepdims=True)
        expd = jnp.exp((sc - top) * 0.125)
        w = expd / jnp.sum(expd, axis=1, keepdims=True)
        w = w.reshape(STEP_USERS * 64, 128)
        same = (iota((128, 128), 0) // 8 == iota((128, 128), 1) // 8).astype(BF16)
        w_hi = w.astype(BF16)
        w_lo = (w - w_hi.astype(F32)).astype(BF16)
        wm = (dot_rows(w_hi, same) + dot_rows(w_lo, same)) * 0.125
        wm = wm.reshape(STEP_USERS * 8, 8, 128)
        on_diag = iota((8, 128), 0) == iota((8, 128), 1) % 8
        row = jnp.sum(jnp.where(on_diag[None], wm, 0.0), axis=1, keepdims=True)
        group_of_lane = iota((TOKENS, 128), 1) // 8 == iota((TOKENS, 128), 0)
        return jnp.where(group_of_lane[None], row, 0.0).astype(BF16)

    def merge(step, x, qkv, spread):
        group_of_lane = iota((TOKENS, 128), 1) // 8 == iota((TOKENS, 128), 0)
        mean_w = jnp.where(group_of_lane, 0.125, 0.0).astype(BF16)
        low_half = iota((TOKENS, 128), 1) < 64
        pooled, means = [], []
        for b in range(STEP_USERS):
            rows = slice(b * SPAN, (b + 1) * SPAN)
            tiles = []
            for tp in range(2):
                a = spread[b * 8 + 4 * tp : b * 8 + 4 * tp + 4].reshape(4 * TOKENS, 128)
                r = dot_rows(a, qkv[rows, 1024 + tp * 256 : 1024 + (tp + 1) * 256])
                for t in range(2):
                    cols = slice(t * 128, (t + 1) * 128)
                    at = 2 * t * TOKENS
                    tiles.append(
                        jnp.where(low_half, r[at : at + TOKENS, cols], r[at + TOKENS : at + 2 * TOKENS, cols])
                    )
            pooled.append(jnp.concatenate(tiles, axis=1))
            means.append(dot_rows(mean_w, x[rows]))
        pooled = jnp.concatenate(pooled, axis=0).astype(BF16)

        merged = jnp.concatenate(means, axis=0) + dot_rows(pooled, inner_out_ref[...])
        merged = merged.astype(BF16)
        rows = STEP_USERS * TOKENS
        merged_ref[step * rows : (step + 1) * rows, :] = merged
        normed = norm_f32(merged.astype(F32), merge_gain_ref[...])
        for c in range(4):
            normed_ref[c, step * rows : (step + 1) * rows, :] = normed[:, c * 128 : (c + 1) * 128]

    half = 2 * STEP_USERS
    lane_block = iota((half, 128), 1) // HEAD_DIM

    def pack(step):
        users = slice(step * STEP_USERS, (step + 1) * STEP_USERS)
        first = step * STEP_USERS * TOKENS
        slab_rows = jnp.concatenate(
            [
                jnp.concatenate(
                    [normed_ref[c, pl.ds(first + i, half, stride=8), :] for i in range(8)], axis=0
                ).astype(BF16)
                for c in range(4)
            ],
            axis=1,
        )
        for c in range(3):
            for hp in range(2):
                col = c * 512 + hp * 256
                pair = dot_rows(slab_rows, mixed_qkv_ref[:, col : col + 256])
                if c == 0:
                    pair = pair * SCORE_SCALE
                for ht in (2 * hp, 2 * hp + 1):
                    part = pair[:, (ht % 2) * 128 : (ht % 2 + 1) * 128]
                    for t in range(2):
                        base = [part[(t * 4 + j) * half : (t * 4 + j + 1) * half] for j in range(4)]
                        for hh in range(4):
                            out = None
                            for j in range(4):
                                shift = (HEAD_DIM * (j - hh)) % 128
                                moved = pltpu.roll(base[j], shift, 1) if shift else base[j]
                                out = moved if j == 0 else jnp.where(lane_block == j, moved, out)
                            tile = (c * 2 + t) * 128
                            payload_ref[users, ht * 4 + hh, :, tile : tile + 128] = out.astype(
                                BF16
                            ).reshape(STEP_USERS, 2, 128)

    def pack_globals():
        gnormed = norm_f32(tokens_ref[...].astype(F32), global_gain_ref[...]).astype(BF16)
        block16 = iota((USERS, 128), 1) // HEAD_DIM
        gqkv = [dot_rows(gnormed, mixed_qkv_ref[:, c * 512 : (c + 1) * 512]) for c in range(3)]
        gqkv[0] = gqkv[0] * SCORE_SCALE
        for ht in range(4):
            sect = [part[:, ht * 128 : (ht + 1) * 128] for part in gqkv]
            for hh in range(4):
                out = jnp.zeros((USERS, 128), F32)
                for c in range(3):
                    shift = (HEAD_DIM * (c - hh)) % 128
                    moved = pltpu.roll(sect[c], shift, 1) if shift else sect[c]
                    out = jnp.where(block16 == c, moved, out)
                payload_ref[:, ht * 4 + hh, :, 768:896] = jnp.broadcast_to(
                    out[:, None, :], (USERS, 2, 128)
                ).astype(BF16)

    held, scores, spreads, sent = {}, {}, {}, []
    for turn in range(STEPS + 4):
        if turn < STEPS:
            held[turn] = project(turn)
        if 0 <= turn - 1 < STEPS:
            scores[turn - 1] = score(held[turn - 1][1])
        if 0 <= turn - 2 < STEPS:
            spreads[turn - 2] = pool_weights(scores[turn - 2])
        if 0 <= turn - 3 < STEPS:
            merge(turn - 3, *held[turn - 3], spreads[turn - 3])
        if 0 <= turn - 4 < STEPS:
            pack(turn - 4)
            users = slice((turn - 4) * STEP_USERS, (turn - 3) * STEP_USERS)
            sent.append(
                pltpu.make_async_copy(
                    payload_ref.at[users], payload_hbm.at[users], sems.at[STEPS + 10 + turn - 4]
                )
            )
            sent[-1].start()
        if turn == 0:
            for copy in copies[4:]:
                copy.wait()
        if turn == 1:
            pack_globals()
        if turn == STEPS + 2:
            sent.append(pltpu.make_async_copy(merged_ref, merged_hbm, sems.at[2 * STEPS + 10]))
            sent[-1].start()
    for copy in sent:
        copy.wait()


def inner_call(events, tokens, inner_qkv, inner_out, merge_gain, global_gain, mixed_qkv):
    hbm = pl.BlockSpec(memory_space=pl.ANY)
    return pl.pallas_call(
        inner_kernel,
        in_specs=[hbm] * 7,
        out_specs=[hbm, hbm],
        out_shape=[
            jax.ShapeDtypeStruct((USERS * TOKENS, WIDTH), BF16),
            jax.ShapeDtypeStruct((USERS, HEADS, 2, 896), BF16),
        ],
        scratch_shapes=[
            pltpu.VMEM((USERS * TOKENS, WIDTH), BF16),
            pltpu.VMEM((USERS, HEADS, 2, 896), BF16),
            pltpu.VMEM((4, USERS * TOKENS + PAD, 128), F32),
            pltpu.VMEM((USERS, SPAN, WIDTH), BF16),
            pltpu.VMEM((USERS, WIDTH), BF16),
            pltpu.VMEM((WIDTH, 3 * WIDTH), BF16),
            pltpu.VMEM((WIDTH, WIDTH), BF16),
            pltpu.VMEM((1, WIDTH), F32),
            pltpu.VMEM((1, WIDTH), F32),
            pltpu.VMEM((WIDTH, 3 * WIDTH), BF16),
            pltpu.SemaphoreType.DMA((2 * STEPS + 11,)),
        ],
        compiler_params=pltpu.CompilerParams(vmem_limit_bytes=60 * 2**20),
        name="inner",
    )(events, tokens, inner_qkv, inner_out, merge_gain, global_gain, mixed_qkv)


QT = 512
TILES = COUNT // QT
PR = QT // 8
VROWS = 48
QUERIES = COUNT + GLOBALS


def place(index):
    return (index % PR) * 8 + index // PR


def attend_kernel(lengths_ref, recv_ref, att_ref, glob_ref, qt_ref, k_ref, vt_ref, g_ref, acc_ref):
    valid = lengths_ref[lax.axis_index("seq") // 8] // 8
    same = (iota((128, 128), 0) // HEAD_DIM == iota((128, 128), 1) // HEAD_DIM).astype(BF16)

    def tile_of(index):
        return recv_ref[:, :, index * 128 : (index + 1) * 128].reshape(512, 128)

    g_ref[0:512, :] = tile_of(6).astype(F32)
    g = g_ref[pl.ds(0, GLOBALS, stride=4), :]
    gt = g.T
    gk = pltpu.roll(g, 128 - HEAD_DIM, 1).astype(BF16)[:, :HEAD_DIM]
    qt_ref[:, COUNT:] = gt[:HEAD_DIM].astype(BF16)
    one_row = jnp.where(iota((VROWS - HEAD_DIM, GLOBALS), 0) == 0, 1.0, 0.0)
    gvt = jnp.concatenate([gt[2 * HEAD_DIM : 3 * HEAD_DIM], one_row], axis=0).astype(BF16)
    tail_row = iota((VROWS - HEAD_DIM, 512), 0) == 0
    gg = g * g
    g_sq = dot_rows(gg.astype(BF16), same)
    g_lane = iota((GLOBALS, 128), 1) // HEAD_DIM
    k_top = jnp.max(jnp.where(g_lane == 1, g_sq, 0.0))

    for t in range(2):
        q_t = tile_of(t).astype(F32).T.astype(BF16)
        for j in range(4):
            band = slice(j * HEAD_DIM, (j + 1) * HEAD_DIM)
            for n in range(TILES):
                at = n * QT + (t * 4 + j) * PR
                qt_ref[:, at : at + PR] = q_t[band, n * PR : (n + 1) * PR]

    def finish():
        acc = acc_ref[...]
        o = acc[:HEAD_DIM] / acc[HEAD_DIM : HEAD_DIM + 1]
        glob_ref[...] = o[:, COUNT:].T.astype(BF16)
        for t in range(2):
            bands = []
            for j in range(4):
                at = (t * 4 + j) * PR
                bands.append(
                    jnp.concatenate(
                        [o[:, n * QT + at : n * QT + at + PR] for n in range(TILES)], axis=1
                    )
                )
            packed = jnp.concatenate(bands, axis=0).T.astype(BF16)
            att_ref[:, :, t * 128 : (t + 1) * 128] = packed.reshape(DEVICES, 2, 128)

    acc_ref[...] = dot_rows(gvt, jnp.exp2(dot_rows(gk, qt_ref[...])).astype(BF16))
    causal = place(iota((QT, QT), 1)) >= place(iota((QT, QT), 0))
    v_t = [tile_of(4 + t).astype(F32).T for t in range(2)]
    k_packed = [tile_of(2 + t).astype(F32) for t in range(2)]
    for m in range(TILES):
        lo, hi = m * QT, (m + 1) * QT
        part = slice(m * PR, (m + 1) * PR)
        keys, vals = [], []
        for t in range(2):
            k = k_packed[t][part]
            for j in range(4):
                keys.append(pltpu.roll(k, 128 - j * HEAD_DIM, 1) if j else k)
                vals.append(v_t[t][j * HEAD_DIM : (j + 1) * HEAD_DIM, part])
        k = jnp.concatenate(keys, axis=0).astype(BF16)
        live = place(iota((HEAD_DIM, QT), 1)) + lo < valid
        v = jnp.where(live, jnp.concatenate(vals, axis=1), 0.0)
        tail = jnp.where(tail_row & live[: VROWS - HEAD_DIM], 1.0, 0.0)
        v = jnp.concatenate([v, tail], axis=0).astype(BF16)
        k_ref[lo:hi, :] = k
        vt_ref[m] = v
        k = k[:, :HEAD_DIM]
        p = jnp.exp2(dot_rows(k, qt_ref[:, lo:]))
        p = jnp.concatenate([jnp.where(causal, p[:, :QT], 0.0), p[:, QT:]], axis=1)
        acc_ref[:, lo:] += dot_rows(v, p.astype(BF16))
    finish()

    q_all = qt_ref[...].astype(F32)
    q_top = jnp.max(jnp.sum(q_all * q_all, axis=0, keepdims=True))
    for t in range(2):
        k = k_packed[t]
        k_top = jnp.maximum(k_top, jnp.max(dot_rows((k * k).astype(BF16), same)))
    safe = q_top * k_top * 1.05 < SAFE * SAFE

    @pl.when(jnp.logical_not(safe))
    def _():
        lane = iota((QT, QUERIES), 1)
        q_at = jnp.where(lane < COUNT, lane // QT * QT + place(lane % QT), COUNT)
        k_at = place(iota((QT, QUERIES), 0))
        s = dot_rows(gk, qt_ref[...])
        top = jnp.max(s, axis=0, keepdims=True)
        acc_ref[...] = dot_rows(gvt, jnp.exp2(s - top).astype(BF16))

        def body(m, top):
            at = pl.multiple_of(m * QT, QT)
            s = dot_rows(k_ref[pl.ds(at, QT), :][:, :HEAD_DIM], qt_ref[...])
            key = k_at + m * QT
            s = jnp.where((key <= q_at) & (key < valid), s, LOW)
            new = jnp.maximum(top, jnp.max(s, axis=0, keepdims=True))
            p = jnp.exp2(s - new).astype(BF16)
            acc_ref[...] = acc_ref[...] * jnp.exp2(top - new) + dot_rows(vt_ref[m], p)
            return new

        lax.fori_loop(0, TILES, body, top)
        finish()


def attend_call(lengths, recv):
    vmem = pl.BlockSpec(memory_space=pltpu.VMEM)
    return pl.pallas_call(
        attend_kernel,
        in_specs=[pl.BlockSpec(memory_space=pltpu.SMEM), vmem],
        out_specs=[vmem, vmem],
        out_shape=[
            jax.ShapeDtypeStruct((DEVICES, 2, 256), BF16),
            jax.ShapeDtypeStruct((GLOBALS, HEAD_DIM), BF16),
        ],
        scratch_shapes=[
            pltpu.VMEM((HEAD_DIM, QUERIES), BF16),
            pltpu.VMEM((COUNT, 128), BF16),
            pltpu.VMEM((TILES, VROWS, QT), BF16),
            pltpu.VMEM((512 + PAD, 128), F32),
            pltpu.VMEM((VROWS, QUERIES), F32),
        ],
        compiler_params=pltpu.CompilerParams(vmem_limit_bytes=32 * 2**20),
        name="attend",
    )(lengths, recv)


def output_kernel(back_ref, merged_ref, mixed_out_ref, out_ref, wide_ref, sum_ref):
    for h in range(HEADS):
        rows = mixed_out_ref[h * HEAD_DIM : (h + 1) * HEAD_DIM, :]
        for j in range(4):
            wide_ref[h * 128 + j * HEAD_DIM : h * 128 + (j + 1) * HEAD_DIM, :] = rows
    block = iota((2 * USERS, 128), 1) // HEAD_DIM
    keep = [(block == j).astype(F32).astype(BF16) for j in range(4)]
    parts = [[] for _ in range(8)]
    for h in range(HEADS):
        for t in range(2):
            x = back_ref[:, h, :, t * 128 : (t + 1) * 128].reshape(2 * USERS, 128)
            for j in range(4):
                parts[t * 4 + j].append(x * keep[j])
    lhs = jnp.concatenate([jnp.concatenate(p, axis=1) for p in parts], axis=0)
    prod = dot_rows(lhs, wide_ref[...])
    for c in range(4):
        cols = slice(c * 128, (c + 1) * 128)
        for i in range(8):
            rows = slice(i * 2 * USERS, (i + 1) * 2 * USERS)
            sum_ref[c, pl.ds(i, 2 * USERS, stride=8), :] = prod[rows, cols]
        out_ref[:, cols] = (merged_ref[:, cols].astype(F32) + sum_ref[c, : USERS * TOKENS]).astype(BF16)


def output_call(back, merged, mixed_out):
    vmem = pl.BlockSpec(memory_space=pltpu.VMEM)
    return pl.pallas_call(
        output_kernel,
        in_specs=[vmem] * 3,
        out_specs=vmem,
        out_shape=jax.ShapeDtypeStruct((USERS * TOKENS, WIDTH), BF16),
        scratch_shapes=[
            pltpu.VMEM((HEADS * 128, WIDTH), BF16),
            pltpu.VMEM((4, USERS * TOKENS + PAD, 128), F32),
        ],
        compiler_params=pltpu.CompilerParams(vmem_limit_bytes=16 * 2**20),
        name="output",
    )(back, merged, mixed_out)


def per_device(
    events,
    global_tokens,
    lengths,
    inner_qkv,
    inner_out,
    merge_gain,
    global_gain,
    mixed_qkv,
    mixed_out,
):
    merged, payload = inner_call(
        events,
        global_tokens.reshape(USERS, WIDTH),
        inner_qkv,
        inner_out,
        merge_gain.reshape(1, WIDTH),
        global_gain.reshape(1, WIDTH),
        mixed_qkv,
    )
    arrived = lax.all_to_all(
        payload.reshape(DEVICES, 2, 896), ("seq", "head"), split_axis=0, concat_axis=0, tiled=True
    )
    att, glob = attend_call(lengths, arrived)
    back = lax.all_to_all(att, ("seq", "head"), split_axis=0, concat_axis=0, tiled=True)
    out = output_call(back.reshape(USERS, HEADS, 2, 256), merged, mixed_out)
    return (out.reshape(USERS, TOKENS, WIDTH), glob.reshape(1, 1, GLOBALS * HEAD_DIM))


def solution(mesh):
    in_specs = (
        P(None, ("seq", "head"), None),
        P(None, "seq", None),
        P(),
        P(),
        P(),
        P(),
        P(),
        P(),
        P(),
    )
    out_specs = (P(None, ("seq", "head"), None), P("seq", "head", None))
    return jax.shard_map(
        per_device, mesh=mesh, in_specs=in_specs, out_specs=out_specs, check_vma=False
    )
```

```python
import functools
import math

import jax
import jax.numpy as jnp
from jax import lax
from jax.experimental import pallas as pl
from jax.experimental.pallas import tpu as pltpu
from jax.sharding import PartitionSpec as P

BF16 = jnp.bfloat16
F32 = jnp.float32
USERS = 16
HEADS = 16
WIDTH = 512
HEAD_DIM = 32
GLOBALS = 128
SPAN = 128
TOKENS = 16
DEVICES = 256
COUNT = DEVICES * TOKENS
STEP_USERS = 8
STEPS = USERS // STEP_USERS
SCORE_SCALE = math.log2(math.e) / math.sqrt(HEAD_DIM)
SAFE = 100.0
LOW = -1e30
PAD = 8


def dot_rows(a, b):
    return lax.dot_general(a, b, (((1,), (0,)), ((), ())), preferred_element_type=F32)


def dot_last(a, b):
    return lax.dot_general(a, b, (((1,), (1,)), ((), ())), preferred_element_type=F32)


def iota(shape, axis):
    return lax.broadcasted_iota(jnp.int32, shape, axis)


def norm_f32(wide, gain):
    scale = lax.rsqrt(jnp.mean(wide * wide, axis=-1, keepdims=True) + 1e-06)
    return wide * scale * gain


def inner_kernel(
    events_hbm,
    tokens_hbm,
    inner_qkv_hbm,
    inner_out_hbm,
    merge_gain_hbm,
    global_gain_hbm,
    mixed_qkv_hbm,
    merged_hbm,
    payload_hbm,
    merged_ref,
    payload_ref,
    normed_ref,
    events_ref,
    tokens_ref,
    inner_qkv_ref,
    inner_out_ref,
    merge_gain_ref,
    global_gain_ref,
    mixed_qkv_ref,
    sems,
):
    fetch = [(events_hbm.at[0:STEP_USERS], events_ref.at[0:STEP_USERS])]
    for c in range(3):
        cols = slice(c * WIDTH, (c + 1) * WIDTH)
        fetch.append((inner_qkv_hbm.at[:, cols], inner_qkv_ref.at[:, cols]))
    for n in range(1, STEPS):
        users = slice(n * STEP_USERS, (n + 1) * STEP_USERS)
        fetch.append((events_hbm.at[users], events_ref.at[users]))
    fetch.append((inner_out_hbm, inner_out_ref))
    fetch.append((merge_gain_hbm, merge_gain_ref))
    for c in range(3):
        cols = slice(c * WIDTH, (c + 1) * WIDTH)
        fetch.append((mixed_qkv_hbm.at[:, cols], mixed_qkv_ref.at[:, cols]))
    fetch.append((tokens_hbm, tokens_ref))
    fetch.append((global_gain_hbm, global_gain_ref))
    copies = [
        pltpu.make_async_copy(src, dst, sems.at[n]) for n, (src, dst) in enumerate(fetch)
    ]
    for copy in copies[:4]:
        copy.start()

    lane = iota((SPAN, 128), 1)
    low = (lane < 64).astype(F32).astype(BF16)
    high = (lane >= 64).astype(F32).astype(BF16)
    lane_group8 = iota((8, 128), 1) // 8

    def project(step):
        if step == 0:
            copies[0].wait()
        x = events_ref[step * STEP_USERS : (step + 1) * STEP_USERS]
        x = x.reshape(STEP_USERS * SPAN, WIDTH)
        if step == 0:
            for copy in copies[1:4]:
                copy.wait()
            for copy in copies[4:]:
                copy.start()
        return x, dot_rows(x, inner_qkv_ref[...]).astype(BF16)

    def score(qkv):
        compact = []
        for b in range(STEP_USERS):
            rows = slice(b * SPAN, (b + 1) * SPAN)
            for t in range(4):
                q = qkv[rows, t * 128 : (t + 1) * 128]
                k = qkv[rows, 512 + t * 128 : 512 + (t + 1) * 128]
                scores = dot_last(k, jnp.concatenate([q * low, q * high], axis=0))
                for half in range(2):
                    part = scores[:, half * 128 : (half + 1) * 128]
                    picked = part[0:8]
                    for g in range(1, TOKENS):
                        picked = jnp.where(lane_group8 == g, part[g * 8 : g * 8 + 8], picked)
                    compact.append(picked)
        return jnp.stack(compact, axis=0)

    def pool_weights(sc):
        top = jnp.max(sc, axis=1, keepdims=True)
        expd = jnp.exp((sc - top) * 0.125)
        w = expd / jnp.sum(expd, axis=1, keepdims=True)
        w = w.reshape(STEP_USERS * 64, 128)
        same = (iota((128, 128), 0) // 8 == iota((128, 128), 1) // 8).astype(BF16)
        w_hi = w.astype(BF16)
        w_lo = (w - w_hi.astype(F32)).astype(BF16)
        wm = (dot_rows(w_hi, same) + dot_rows(w_lo, same)) * 0.125
        wm = wm.reshape(STEP_USERS * 8, 8, 128)
        on_diag = iota((8, 128), 0) == iota((8, 128), 1) % 8
        row = jnp.sum(jnp.where(on_diag[None], wm, 0.0), axis=1, keepdims=True)
        group_of_lane = iota((TOKENS, 128), 1) // 8 == iota((TOKENS, 128), 0)
        return jnp.where(group_of_lane[None], row, 0.0).astype(BF16)

    def merge(step, x, qkv, spread):
        group_of_lane = iota((TOKENS, 128), 1) // 8 == iota((TOKENS, 128), 0)
        mean_w = jnp.where(group_of_lane, 0.125, 0.0).astype(BF16)
        low_half = iota((TOKENS, 128), 1) < 64
        pooled, means = [], []
        for b in range(STEP_USERS):
            rows = slice(b * SPAN, (b + 1) * SPAN)
            tiles = []
            for tp in range(2):
                a = spread[b * 8 + 4 * tp : b * 8 + 4 * tp + 4].reshape(4 * TOKENS, 128)
                r = dot_rows(a, qkv[rows, 1024 + tp * 256 : 1024 + (tp + 1) * 256])
                for t in range(2):
                    cols = slice(t * 128, (t + 1) * 128)
                    at = 2 * t * TOKENS
                    tiles.append(
                        jnp.where(low_half, r[at : at + TOKENS, cols], r[at + TOKENS : at + 2 * TOKENS, cols])
                    )
            pooled.append(jnp.concatenate(tiles, axis=1))
            means.append(dot_rows(mean_w, x[rows]))
        pooled = jnp.concatenate(pooled, axis=0).astype(BF16)

        merged = jnp.concatenate(means, axis=0) + dot_rows(pooled, inner_out_ref[...])
        merged = merged.astype(BF16)
        rows = STEP_USERS * TOKENS
        merged_ref[step * rows : (step + 1) * rows, :] = merged
        normed = norm_f32(merged.astype(F32), merge_gain_ref[...])
        for c in range(4):
            normed_ref[c, step * rows : (step + 1) * rows, :] = normed[:, c * 128 : (c + 1) * 128]

    half = 2 * STEP_USERS
    lane_block = iota((half, 128), 1) // HEAD_DIM

    def pack(step):
        users = slice(step * STEP_USERS, (step + 1) * STEP_USERS)
        first = step * STEP_USERS * TOKENS
        slab_rows = jnp.concatenate(
            [
                jnp.concatenate(
                    [normed_ref[c, pl.ds(first + i, half, stride=8), :] for i in range(8)], axis=0
                ).astype(BF16)
                for c in range(4)
            ],
            axis=1,
        )
        for c in range(3):
            for hp in range(2):
                col = c * 512 + hp * 256
                pair = dot_rows(slab_rows, mixed_qkv_ref[:, col : col + 256])
                if c == 0:
                    pair = pair * SCORE_SCALE
                for ht in (2 * hp, 2 * hp + 1):
                    part = pair[:, (ht % 2) * 128 : (ht % 2 + 1) * 128]
                    for t in range(2):
                        base = [part[(t * 4 + j) * half : (t * 4 + j + 1) * half] for j in range(4)]
                        for hh in range(4):
                            out = None
                            for j in range(4):
                                shift = (HEAD_DIM * (j - hh)) % 128
                                moved = pltpu.roll(base[j], shift, 1) if shift else base[j]
                                out = moved if j == 0 else jnp.where(lane_block == j, moved, out)
                            tile = (c * 2 + t) * 128
                            payload_ref[users, ht * 4 + hh, :, tile : tile + 128] = out.astype(
                                BF16
                            ).reshape(STEP_USERS, 2, 128)

    def pack_globals():
        gnormed = norm_f32(tokens_ref[...].astype(F32), global_gain_ref[...]).astype(BF16)
        block16 = iota((USERS, 128), 1) // HEAD_DIM
        gqkv = [dot_rows(gnormed, mixed_qkv_ref[:, c * 512 : (c + 1) * 512]) for c in range(3)]
        gqkv[0] = gqkv[0] * SCORE_SCALE
        for ht in range(4):
            sect = [part[:, ht * 128 : (ht + 1) * 128] for part in gqkv]
            for hh in range(4):
                out = jnp.zeros((USERS, 128), F32)
                for c in range(3):
                    shift = (HEAD_DIM * (c - hh)) % 128
                    moved = pltpu.roll(sect[c], shift, 1) if shift else sect[c]
                    out = jnp.where(block16 == c, moved, out)
                payload_ref[:, ht * 4 + hh, :, 768:896] = jnp.broadcast_to(
                    out[:, None, :], (USERS, 2, 128)
                ).astype(BF16)

    held, scores, spreads, sent = {}, {}, {}, []
    for turn in range(STEPS + 4):
        if turn < STEPS:
            held[turn] = project(turn)
        if 0 <= turn - 1 < STEPS:
            scores[turn - 1] = score(held[turn - 1][1])
        if 0 <= turn - 2 < STEPS:
            spreads[turn - 2] = pool_weights(scores[turn - 2])
        if 0 <= turn - 3 < STEPS:
            merge(turn - 3, *held[turn - 3], spreads[turn - 3])
        if 0 <= turn - 4 < STEPS:
            pack(turn - 4)
            users = slice((turn - 4) * STEP_USERS, (turn - 3) * STEP_USERS)
            sent.append(
                pltpu.make_async_copy(
                    payload_ref.at[users], payload_hbm.at[users], sems.at[STEPS + 10 + turn - 4]
                )
            )
            sent[-1].start()
        if turn == 0:
            for copy in copies[4:]:
                copy.wait()
        if turn == 1:
            pack_globals()
        if turn == STEPS + 2:
            sent.append(pltpu.make_async_copy(merged_ref, merged_hbm, sems.at[2 * STEPS + 10]))
            sent[-1].start()
    for copy in sent:
        copy.wait()


def inner_call(events, tokens, inner_qkv, inner_out, merge_gain, global_gain, mixed_qkv):
    hbm = pl.BlockSpec(memory_space=pl.ANY)
    return pl.pallas_call(
        inner_kernel,
        in_specs=[hbm] * 7,
        out_specs=[hbm, hbm],
        out_shape=[
            jax.ShapeDtypeStruct((USERS * TOKENS, WIDTH), BF16),
            jax.ShapeDtypeStruct((USERS, HEADS, 2, 896), BF16),
        ],
        scratch_shapes=[
            pltpu.VMEM((USERS * TOKENS, WIDTH), BF16),
            pltpu.VMEM((USERS, HEADS, 2, 896), BF16),
            pltpu.VMEM((4, USERS * TOKENS + PAD, 128), F32),
            pltpu.VMEM((USERS, SPAN, WIDTH), BF16),
            pltpu.VMEM((USERS, WIDTH), BF16),
            pltpu.VMEM((WIDTH, 3 * WIDTH), BF16),
            pltpu.VMEM((WIDTH, WIDTH), BF16),
            pltpu.VMEM((1, WIDTH), F32),
            pltpu.VMEM((1, WIDTH), F32),
            pltpu.VMEM((WIDTH, 3 * WIDTH), BF16),
            pltpu.SemaphoreType.DMA((2 * STEPS + 11,)),
        ],
        compiler_params=pltpu.CompilerParams(vmem_limit_bytes=60 * 2**20),
        name="inner",
    )(events, tokens, inner_qkv, inner_out, merge_gain, global_gain, mixed_qkv)


QT = 512
TILES = COUNT // QT
PR = QT // 8
VROWS = 48
QUERIES = COUNT + GLOBALS


def place(index):
    return (index % PR) * 8 + index // PR


def attend_kernel(lengths_ref, recv_ref, att_ref, glob_ref, qt_ref, k_ref, vt_ref, g_ref, acc_ref):
    valid = lengths_ref[lax.axis_index("seq") // 8] // 8
    same = (iota((128, 128), 0) // HEAD_DIM == iota((128, 128), 1) // HEAD_DIM).astype(BF16)

    def tile_of(index):
        return recv_ref[:, :, index * 128 : (index + 1) * 128].reshape(512, 128)

    g_ref[0:512, :] = tile_of(6).astype(F32)
    g = g_ref[pl.ds(0, GLOBALS, stride=4), :]
    gt = g.T
    gk = pltpu.roll(g, 128 - HEAD_DIM, 1).astype(BF16)[:, :HEAD_DIM]
    qt_ref[:, COUNT:] = gt[:HEAD_DIM].astype(BF16)
    one_row = jnp.where(iota((VROWS - HEAD_DIM, GLOBALS), 0) == 0, 1.0, 0.0)
    gvt = jnp.concatenate([gt[2 * HEAD_DIM : 3 * HEAD_DIM], one_row], axis=0).astype(BF16)
    tail_row = iota((VROWS - HEAD_DIM, 512), 0) == 0
    gg = g * g
    g_sq = dot_rows(gg.astype(BF16), same)
    g_lane = iota((GLOBALS, 128), 1) // HEAD_DIM
    k_top = jnp.max(jnp.where(g_lane == 1, g_sq, 0.0))

    for t in range(2):
        q_t = tile_of(t).astype(F32).T.astype(BF16)
        for j in range(4):
            band = slice(j * HEAD_DIM, (j + 1) * HEAD_DIM)
            for n in range(TILES):
                at = n * QT + (t * 4 + j) * PR
                qt_ref[:, at : at + PR] = q_t[band, n * PR : (n + 1) * PR]

    def finish():
        acc = acc_ref[...]
        o = acc[:HEAD_DIM] / acc[HEAD_DIM : HEAD_DIM + 1]
        g_ref[0:GLOBALS, 0:HEAD_DIM] = o[:, COUNT:].T
        lane = iota((HEAD_DIM, 128), 1) // HEAD_DIM
        rows = g_ref[pl.ds(0, GLOBALS // 4, stride=4), :]
        for n in range(1, 4):
            moved = pltpu.roll(g_ref[pl.ds(n, GLOBALS // 4, stride=4), :], n * HEAD_DIM, 1)
            rows = jnp.where(lane == n, moved, rows)
        for n in range(GLOBALS // 4):
            glob_ref[0, :, n * 128 : (n + 1) * 128] = rows[n : n + 1].astype(BF16)
        for t in range(2):
            bands = []
            for j in range(4):
                at = (t * 4 + j) * PR
                bands.append(
                    jnp.concatenate(
                        [o[:, n * QT + at : n * QT + at + PR] for n in range(TILES)], axis=1
                    )
                )
            packed = jnp.concatenate(bands, axis=0).T.astype(BF16)
            att_ref[:, :, t * 128 : (t + 1) * 128] = packed.reshape(DEVICES, 2, 128)

    acc_ref[...] = dot_rows(gvt, jnp.exp2(dot_rows(gk, qt_ref[...])).astype(BF16))
    causal = place(iota((QT, QT), 1)) >= place(iota((QT, QT), 0))
    v_t = [tile_of(4 + t).astype(F32).T for t in range(2)]
    k_packed = [tile_of(2 + t).astype(F32) for t in range(2)]
    for m in range(TILES):
        lo, hi = m * QT, (m + 1) * QT
        part = slice(m * PR, (m + 1) * PR)
        keys, vals = [], []
        for t in range(2):
            k = k_packed[t][part]
            for j in range(4):
                keys.append(pltpu.roll(k, 128 - j * HEAD_DIM, 1) if j else k)
                vals.append(v_t[t][j * HEAD_DIM : (j + 1) * HEAD_DIM, part])
        k = jnp.concatenate(keys, axis=0).astype(BF16)
        live = place(iota((HEAD_DIM, QT), 1)) + lo < valid
        v = jnp.where(live, jnp.concatenate(vals, axis=1), 0.0)
        tail = jnp.where(tail_row & live[: VROWS - HEAD_DIM], 1.0, 0.0)
        v = jnp.concatenate([v, tail], axis=0).astype(BF16)
        k_ref[lo:hi, :] = k
        vt_ref[m] = v
        k = k[:, :HEAD_DIM]
        p = jnp.exp2(dot_rows(k, qt_ref[:, lo:]))
        p = jnp.concatenate([jnp.where(causal, p[:, :QT], 0.0), p[:, QT:]], axis=1)
        acc_ref[:, lo:] += dot_rows(v, p.astype(BF16))
    finish()

    q_all = qt_ref[...].astype(F32)
    q_top = jnp.max(jnp.sum(q_all * q_all, axis=0, keepdims=True))
    for t in range(2):
        k = k_packed[t]
        k_top = jnp.maximum(k_top, jnp.max(dot_rows((k * k).astype(BF16), same)))
    safe = q_top * k_top * 1.05 < SAFE * SAFE

    @pl.when(jnp.logical_not(safe))
    def _():
        lane = iota((QT, QUERIES), 1)
        q_at = jnp.where(lane < COUNT, lane // QT * QT + place(lane % QT), COUNT)
        k_at = place(iota((QT, QUERIES), 0))
        s = dot_rows(gk, qt_ref[...])
        top = jnp.max(s, axis=0, keepdims=True)
        acc_ref[...] = dot_rows(gvt, jnp.exp2(s - top).astype(BF16))

        def body(m, top):
            at = pl.multiple_of(m * QT, QT)
            s = dot_rows(k_ref[pl.ds(at, QT), :][:, :HEAD_DIM], qt_ref[...])
            key = k_at + m * QT
            s = jnp.where((key <= q_at) & (key < valid), s, LOW)
            new = jnp.maximum(top, jnp.max(s, axis=0, keepdims=True))
            p = jnp.exp2(s - new).astype(BF16)
            acc_ref[...] = acc_ref[...] * jnp.exp2(top - new) + dot_rows(vt_ref[m], p)
            return new

        lax.fori_loop(0, TILES, body, top)
        finish()


def attend_call(lengths, recv):
    vmem = pl.BlockSpec(memory_space=pltpu.VMEM)
    return pl.pallas_call(
        attend_kernel,
        in_specs=[pl.BlockSpec(memory_space=pltpu.SMEM), vmem],
        out_specs=[vmem, vmem],
        out_shape=[
            jax.ShapeDtypeStruct((DEVICES, 2, 256), BF16),
            jax.ShapeDtypeStruct((1, 1, GLOBALS * HEAD_DIM), BF16),
        ],
        scratch_shapes=[
            pltpu.VMEM((HEAD_DIM, QUERIES), BF16),
            pltpu.VMEM((COUNT, 128), BF16),
            pltpu.VMEM((TILES, VROWS, QT), BF16),
            pltpu.VMEM((512 + PAD, 128), F32),
            pltpu.VMEM((VROWS, QUERIES), F32),
        ],
        compiler_params=pltpu.CompilerParams(vmem_limit_bytes=32 * 2**20),
        name="attend",
    )(lengths, recv)


def output_kernel(back_ref, merged_ref, mixed_out_ref, out_ref, wide_ref, sum_ref):
    for h in range(HEADS):
        rows = mixed_out_ref[h * HEAD_DIM : (h + 1) * HEAD_DIM, :]
        for j in range(4):
            wide_ref[h * 128 + j * HEAD_DIM : h * 128 + (j + 1) * HEAD_DIM, :] = rows
    block = iota((2 * USERS, 128), 1) // HEAD_DIM
    keep = [(block == j).astype(F32).astype(BF16) for j in range(4)]
    parts = [[] for _ in range(8)]
    for h in range(HEADS):
        for t in range(2):
            x = back_ref[:, h, :, t * 128 : (t + 1) * 128].reshape(2 * USERS, 128)
            for j in range(4):
                parts[t * 4 + j].append(x * keep[j])
    lhs = jnp.concatenate([jnp.concatenate(p, axis=1) for p in parts], axis=0)
    prod = dot_rows(lhs, wide_ref[...])
    for c in range(4):
        cols = slice(c * 128, (c + 1) * 128)
        for i in range(8):
            rows = slice(i * 2 * USERS, (i + 1) * 2 * USERS)
            sum_ref[c, pl.ds(i, 2 * USERS, stride=8), :] = prod[rows, cols]
        out_ref[:, cols] = (merged_ref[:, cols].astype(F32) + sum_ref[c, : USERS * TOKENS]).astype(BF16)


def output_call(back, merged, mixed_out):
    vmem = pl.BlockSpec(memory_space=pltpu.VMEM)
    return pl.pallas_call(
        output_kernel,
        in_specs=[vmem] * 3,
        out_specs=vmem,
        out_shape=jax.ShapeDtypeStruct((USERS * TOKENS, WIDTH), BF16),
        scratch_shapes=[
            pltpu.VMEM((HEADS * 128, WIDTH), BF16),
            pltpu.VMEM((4, USERS * TOKENS + PAD, 128), F32),
        ],
        compiler_params=pltpu.CompilerParams(vmem_limit_bytes=16 * 2**20),
        name="output",
    )(back, merged, mixed_out)


def per_device(
    events,
    global_tokens,
    lengths,
    inner_qkv,
    inner_out,
    merge_gain,
    global_gain,
    mixed_qkv,
    mixed_out,
):
    merged, payload = inner_call(
        events,
        global_tokens.reshape(USERS, WIDTH),
        inner_qkv,
        inner_out,
        merge_gain.reshape(1, WIDTH),
        global_gain.reshape(1, WIDTH),
        mixed_qkv,
    )
    arrived = lax.all_to_all(
        payload.reshape(DEVICES, 2, 896), ("seq", "head"), split_axis=0, concat_axis=0, tiled=True
    )
    att, glob = attend_call(lengths, arrived)
    back = lax.all_to_all(att, ("seq", "head"), split_axis=0, concat_axis=0, tiled=True)
    out = output_call(back.reshape(USERS, HEADS, 2, 256), merged, mixed_out)
    return (out.reshape(USERS, TOKENS, WIDTH), glob)


def solution(mesh):
    in_specs = (
        P(None, ("seq", "head"), None),
        P(None, "seq", None),
        P(),
        P(),
        P(),
        P(),
        P(),
        P(),
        P(),
    )
    out_specs = (P(None, ("seq", "head"), None), P("seq", "head", None))
    return jax.shard_map(
        per_device, mesh=mesh, in_specs=in_specs, out_specs=out_specs, check_vma=False
    )
```

```python
import functools
import math

import jax
import jax.numpy as jnp
from jax import lax
from jax.experimental import pallas as pl
from jax.experimental.pallas import tpu as pltpu
from jax.sharding import PartitionSpec as P

BF16 = jnp.bfloat16
F32 = jnp.float32
USERS = 16
HEADS = 16
WIDTH = 512
HEAD_DIM = 32
GLOBALS = 128
SPAN = 128
TOKENS = 16
DEVICES = 256
COUNT = DEVICES * TOKENS
STEP_USERS = 8
STEPS = USERS // STEP_USERS
SCORE_SCALE = math.log2(math.e) / math.sqrt(HEAD_DIM)
SAFE = 100.0
LOW = -1e30
PAD = 8


def dot_rows(a, b):
    return lax.dot_general(a, b, (((1,), (0,)), ((), ())), preferred_element_type=F32)


def dot_last(a, b):
    return lax.dot_general(a, b, (((1,), (1,)), ((), ())), preferred_element_type=F32)


def iota(shape, axis):
    return lax.broadcasted_iota(jnp.int32, shape, axis)


def norm_f32(wide, gain):
    scale = lax.rsqrt(jnp.mean(wide * wide, axis=-1, keepdims=True) + 1e-06)
    return wide * scale * gain


def inner_kernel(
    events_hbm,
    tokens_hbm,
    inner_qkv_hbm,
    inner_out_hbm,
    merge_gain_hbm,
    global_gain_hbm,
    mixed_qkv_hbm,
    merged_hbm,
    payload_hbm,
    merged_ref,
    payload_ref,
    normed_ref,
    events_ref,
    tokens_ref,
    inner_qkv_ref,
    inner_out_ref,
    merge_gain_ref,
    global_gain_ref,
    mixed_qkv_ref,
    sems,
):
    fetch = [(events_hbm.at[0:STEP_USERS], events_ref.at[0:STEP_USERS])]
    for c in range(3):
        cols = slice(c * WIDTH, (c + 1) * WIDTH)
        fetch.append((inner_qkv_hbm.at[:, cols], inner_qkv_ref.at[:, cols]))
    for n in range(1, STEPS):
        users = slice(n * STEP_USERS, (n + 1) * STEP_USERS)
        fetch.append((events_hbm.at[users], events_ref.at[users]))
    fetch.append((inner_out_hbm, inner_out_ref))
    fetch.append((merge_gain_hbm, merge_gain_ref))
    for c in range(3):
        cols = slice(c * WIDTH, (c + 1) * WIDTH)
        fetch.append((mixed_qkv_hbm.at[:, cols], mixed_qkv_ref.at[:, cols]))
    fetch.append((tokens_hbm, tokens_ref))
    fetch.append((global_gain_hbm, global_gain_ref))
    copies = [
        pltpu.make_async_copy(src, dst, sems.at[n]) for n, (src, dst) in enumerate(fetch)
    ]
    for copy in copies[:4]:
        copy.start()

    lane = iota((SPAN, 128), 1)
    low = (lane < 64).astype(F32).astype(BF16)
    high = (lane >= 64).astype(F32).astype(BF16)
    lane_group8 = iota((8, 128), 1) // 8

    def project(step):
        if step == 0:
            copies[0].wait()
        x = events_ref[step * STEP_USERS : (step + 1) * STEP_USERS]
        x = x.reshape(STEP_USERS * SPAN, WIDTH)
        if step == 0:
            for copy in copies[1:4]:
                copy.wait()
            for copy in copies[4:]:
                copy.start()
        return x, dot_rows(x, inner_qkv_ref[...]).astype(BF16)

    def score(qkv):
        compact = []
        for b in range(STEP_USERS):
            rows = slice(b * SPAN, (b + 1) * SPAN)
            for t in range(4):
                q = qkv[rows, t * 128 : (t + 1) * 128]
                k = qkv[rows, 512 + t * 128 : 512 + (t + 1) * 128]
                scores = dot_last(k, jnp.concatenate([q * low, q * high], axis=0))
                for half in range(2):
                    part = scores[:, half * 128 : (half + 1) * 128]
                    picked = part[0:8]
                    for g in range(1, TOKENS):
                        picked = jnp.where(lane_group8 == g, part[g * 8 : g * 8 + 8], picked)
                    compact.append(picked)
        return jnp.stack(compact, axis=0)

    def pool_weights(sc):
        top = jnp.max(sc, axis=1, keepdims=True)
        expd = jnp.exp((sc - top) * 0.125)
        w = expd / jnp.sum(expd, axis=1, keepdims=True)
        w = w.reshape(STEP_USERS * 64, 128)
        same = (iota((128, 128), 0) // 8 == iota((128, 128), 1) // 8).astype(BF16)
        wm = dot_rows(w.astype(BF16), same) * 0.125
        wm = wm.reshape(STEP_USERS * 8, 8, 128)
        on_diag = iota((8, 128), 0) == iota((8, 128), 1) % 8
        row = jnp.sum(jnp.where(on_diag[None], wm, 0.0), axis=1, keepdims=True)
        group_of_lane = iota((TOKENS, 128), 1) // 8 == iota((TOKENS, 128), 0)
        return jnp.where(group_of_lane[None], row, 0.0).astype(BF16)

    def merge(step, x, qkv, spread):
        group_of_lane = iota((TOKENS, 128), 1) // 8 == iota((TOKENS, 128), 0)
        mean_w = jnp.where(group_of_lane, 0.125, 0.0).astype(BF16)
        low_half = iota((TOKENS, 128), 1) < 64
        pooled, means = [], []
        for b in range(STEP_USERS):
            rows = slice(b * SPAN, (b + 1) * SPAN)
            tiles = []
            for tp in range(2):
                a = spread[b * 8 + 4 * tp : b * 8 + 4 * tp + 4].reshape(4 * TOKENS, 128)
                r = dot_rows(a, qkv[rows, 1024 + tp * 256 : 1024 + (tp + 1) * 256])
                for t in range(2):
                    cols = slice(t * 128, (t + 1) * 128)
                    at = 2 * t * TOKENS
                    tiles.append(
                        jnp.where(low_half, r[at : at + TOKENS, cols], r[at + TOKENS : at + 2 * TOKENS, cols])
                    )
            pooled.append(jnp.concatenate(tiles, axis=1))
            means.append(dot_rows(mean_w, x[rows]))
        pooled = jnp.concatenate(pooled, axis=0).astype(BF16)

        merged = jnp.concatenate(means, axis=0) + dot_rows(pooled, inner_out_ref[...])
        merged = merged.astype(BF16)
        rows = STEP_USERS * TOKENS
        merged_ref[step * rows : (step + 1) * rows, :] = merged
        normed = norm_f32(merged.astype(F32), merge_gain_ref[...])
        for c in range(4):
            normed_ref[c, step * rows : (step + 1) * rows, :] = normed[:, c * 128 : (c + 1) * 128]

    half = 2 * STEP_USERS
    lane_block = iota((half, 128), 1) // HEAD_DIM

    def pack(step):
        users = slice(step * STEP_USERS, (step + 1) * STEP_USERS)
        first = step * STEP_USERS * TOKENS
        slab_rows = jnp.concatenate(
            [
                jnp.concatenate(
                    [normed_ref[c, pl.ds(first + i, half, stride=8), :] for i in range(8)], axis=0
                ).astype(BF16)
                for c in range(4)
            ],
            axis=1,
        )
        for c in range(3):
            for hp in range(2):
                col = c * 512 + hp * 256
                pair = dot_rows(slab_rows, mixed_qkv_ref[:, col : col + 256])
                if c == 0:
                    pair = pair * SCORE_SCALE
                for ht in (2 * hp, 2 * hp + 1):
                    part = pair[:, (ht % 2) * 128 : (ht % 2 + 1) * 128]
                    for t in range(2):
                        base = [part[(t * 4 + j) * half : (t * 4 + j + 1) * half] for j in range(4)]
                        for hh in range(4):
                            out = None
                            for j in range(4):
                                shift = (HEAD_DIM * (j - hh)) % 128
                                moved = pltpu.roll(base[j], shift, 1) if shift else base[j]
                                out = moved if j == 0 else jnp.where(lane_block == j, moved, out)
                            tile = (c * 2 + t) * 128
                            payload_ref[users, ht * 4 + hh, :, tile : tile + 128] = out.astype(
                                BF16
                            ).reshape(STEP_USERS, 2, 128)

    def pack_globals():
        gnormed = norm_f32(tokens_ref[...].astype(F32), global_gain_ref[...]).astype(BF16)
        block16 = iota((USERS, 128), 1) // HEAD_DIM
        gqkv = [dot_rows(gnormed, mixed_qkv_ref[:, c * 512 : (c + 1) * 512]) for c in range(3)]
        gqkv[0] = gqkv[0] * SCORE_SCALE
        for ht in range(4):
            sect = [part[:, ht * 128 : (ht + 1) * 128] for part in gqkv]
            for hh in range(4):
                out = jnp.zeros((USERS, 128), F32)
                for c in range(3):
                    shift = (HEAD_DIM * (c - hh)) % 128
                    moved = pltpu.roll(sect[c], shift, 1) if shift else sect[c]
                    out = jnp.where(block16 == c, moved, out)
                payload_ref[:, ht * 4 + hh, :, 768:896] = jnp.broadcast_to(
                    out[:, None, :], (USERS, 2, 128)
                ).astype(BF16)

    held, scores, spreads, sent = {}, {}, {}, []
    for turn in range(STEPS + 4):
        if turn < STEPS:
            held[turn] = project(turn)
        if 0 <= turn - 1 < STEPS:
            scores[turn - 1] = score(held[turn - 1][1])
        if 0 <= turn - 2 < STEPS:
            spreads[turn - 2] = pool_weights(scores[turn - 2])
        if 0 <= turn - 3 < STEPS:
            merge(turn - 3, *held[turn - 3], spreads[turn - 3])
        if 0 <= turn - 4 < STEPS:
            pack(turn - 4)
            users = slice((turn - 4) * STEP_USERS, (turn - 3) * STEP_USERS)
            sent.append(
                pltpu.make_async_copy(
                    payload_ref.at[users], payload_hbm.at[users], sems.at[STEPS + 10 + turn - 4]
                )
            )
            sent[-1].start()
        if turn == 0:
            for copy in copies[4:]:
                copy.wait()
        if turn == 1:
            pack_globals()
        if turn == STEPS + 2:
            sent.append(pltpu.make_async_copy(merged_ref, merged_hbm, sems.at[2 * STEPS + 10]))
            sent[-1].start()
    for copy in sent:
        copy.wait()


def inner_call(events, tokens, inner_qkv, inner_out, merge_gain, global_gain, mixed_qkv):
    hbm = pl.BlockSpec(memory_space=pl.ANY)
    return pl.pallas_call(
        inner_kernel,
        in_specs=[hbm] * 7,
        out_specs=[hbm, hbm],
        out_shape=[
            jax.ShapeDtypeStruct((USERS * TOKENS, WIDTH), BF16),
            jax.ShapeDtypeStruct((USERS, HEADS, 2, 896), BF16),
        ],
        scratch_shapes=[
            pltpu.VMEM((USERS * TOKENS, WIDTH), BF16),
            pltpu.VMEM((USERS, HEADS, 2, 896), BF16),
            pltpu.VMEM((4, USERS * TOKENS + PAD, 128), F32),
            pltpu.VMEM((USERS, SPAN, WIDTH), BF16),
            pltpu.VMEM((USERS, WIDTH), BF16),
            pltpu.VMEM((WIDTH, 3 * WIDTH), BF16),
            pltpu.VMEM((WIDTH, WIDTH), BF16),
            pltpu.VMEM((1, WIDTH), F32),
            pltpu.VMEM((1, WIDTH), F32),
            pltpu.VMEM((WIDTH, 3 * WIDTH), BF16),
            pltpu.SemaphoreType.DMA((2 * STEPS + 11,)),
        ],
        compiler_params=pltpu.CompilerParams(vmem_limit_bytes=60 * 2**20),
        name="inner",
    )(events, tokens, inner_qkv, inner_out, merge_gain, global_gain, mixed_qkv)


QT = 512
TILES = COUNT // QT
PR = QT // 8
VROWS = 48
QUERIES = COUNT + GLOBALS


def place(index):
    return (index % PR) * 8 + index // PR


def attend_kernel(lengths_ref, recv_ref, att_ref, glob_ref, qt_ref, k_ref, vt_ref, g_ref, acc_ref):
    valid = lengths_ref[lax.axis_index("seq") // 8] // 8
    same = (iota((128, 128), 0) // HEAD_DIM == iota((128, 128), 1) // HEAD_DIM).astype(BF16)

    def tile_of(index):
        return recv_ref[:, :, index * 128 : (index + 1) * 128].reshape(512, 128)

    g_ref[0:512, :] = tile_of(6).astype(F32)
    g = g_ref[pl.ds(0, GLOBALS, stride=4), :]
    gt = g.T
    gk = pltpu.roll(g, 128 - HEAD_DIM, 1).astype(BF16)[:, :HEAD_DIM]
    qt_ref[:, COUNT:] = gt[:HEAD_DIM].astype(BF16)
    one_row = jnp.where(iota((VROWS - HEAD_DIM, GLOBALS), 0) == 0, 1.0, 0.0)
    gvt = jnp.concatenate([gt[2 * HEAD_DIM : 3 * HEAD_DIM], one_row], axis=0).astype(BF16)
    tail_row = iota((VROWS - HEAD_DIM, 512), 0) == 0
    gg = g * g
    g_sq = dot_rows(gg.astype(BF16), same)
    g_lane = iota((GLOBALS, 128), 1) // HEAD_DIM
    k_top = jnp.max(jnp.where(g_lane == 1, g_sq, 0.0))

    for t in range(2):
        q_t = tile_of(t).astype(F32).T.astype(BF16)
        for j in range(4):
            band = slice(j * HEAD_DIM, (j + 1) * HEAD_DIM)
            for n in range(TILES):
                at = n * QT + (t * 4 + j) * PR
                qt_ref[:, at : at + PR] = q_t[band, n * PR : (n + 1) * PR]

    def finish():
        acc = acc_ref[...]
        o = acc[:HEAD_DIM] / acc[HEAD_DIM : HEAD_DIM + 1]
        g_ref[0:GLOBALS, 0:HEAD_DIM] = o[:, COUNT:].T
        lane = iota((HEAD_DIM, 128), 1) // HEAD_DIM
        rows = g_ref[pl.ds(0, GLOBALS // 4, stride=4), :]
        for n in range(1, 4):
            moved = pltpu.roll(g_ref[pl.ds(n, GLOBALS // 4, stride=4), :], n * HEAD_DIM, 1)
            rows = jnp.where(lane == n, moved, rows)
        for n in range(GLOBALS // 4):
            glob_ref[0, :, n * 128 : (n + 1) * 128] = rows[n : n + 1].astype(BF16)
        for t in range(2):
            bands = []
            for j in range(4):
                at = (t * 4 + j) * PR
                bands.append(
                    jnp.concatenate(
                        [o[:, n * QT + at : n * QT + at + PR] for n in range(TILES)], axis=1
                    )
                )
            packed = jnp.concatenate(bands, axis=0).T.astype(BF16)
            att_ref[:, :, t * 128 : (t + 1) * 128] = packed.reshape(DEVICES, 2, 128)

    acc_ref[...] = dot_rows(gvt, jnp.exp2(dot_rows(gk, qt_ref[...])).astype(BF16))
    causal = place(iota((QT, QT), 1)) >= place(iota((QT, QT), 0))
    v_t = [tile_of(4 + t).astype(F32).T for t in range(2)]
    k_packed = [tile_of(2 + t).astype(F32) for t in range(2)]
    for m in range(TILES):
        lo, hi = m * QT, (m + 1) * QT
        part = slice(m * PR, (m + 1) * PR)
        keys, vals = [], []
        for t in range(2):
            k = k_packed[t][part]
            for j in range(4):
                keys.append(pltpu.roll(k, 128 - j * HEAD_DIM, 1) if j else k)
                vals.append(v_t[t][j * HEAD_DIM : (j + 1) * HEAD_DIM, part])
        k = jnp.concatenate(keys, axis=0).astype(BF16)
        live = place(iota((HEAD_DIM, QT), 1)) + lo < valid
        v = jnp.where(live, jnp.concatenate(vals, axis=1), 0.0)
        tail = jnp.where(tail_row & live[: VROWS - HEAD_DIM], 1.0, 0.0)
        v = jnp.concatenate([v, tail], axis=0).astype(BF16)
        k_ref[lo:hi, :] = k
        vt_ref[m] = v
        k = k[:, :HEAD_DIM]
        p = jnp.exp2(dot_rows(k, qt_ref[:, lo:]))
        p = jnp.concatenate([jnp.where(causal, p[:, :QT], 0.0), p[:, QT:]], axis=1)
        acc_ref[:, lo:] += dot_rows(v, p.astype(BF16))
    finish()

    q_all = qt_ref[...].astype(F32)
    q_top = jnp.max(jnp.sum(q_all * q_all, axis=0, keepdims=True))
    for t in range(2):
        k = k_packed[t]
        k_top = jnp.maximum(k_top, jnp.max(dot_rows((k * k).astype(BF16), same)))
    safe = q_top * k_top * 1.05 < SAFE * SAFE

    @pl.when(jnp.logical_not(safe))
    def _():
        lane = iota((QT, QUERIES), 1)
        q_at = jnp.where(lane < COUNT, lane // QT * QT + place(lane % QT), COUNT)
        k_at = place(iota((QT, QUERIES), 0))
        s = dot_rows(gk, qt_ref[...])
        top = jnp.max(s, axis=0, keepdims=True)
        acc_ref[...] = dot_rows(gvt, jnp.exp2(s - top).astype(BF16))

        def body(m, top):
            at = pl.multiple_of(m * QT, QT)
            s = dot_rows(k_ref[pl.ds(at, QT), :][:, :HEAD_DIM], qt_ref[...])
            key = k_at + m * QT
            s = jnp.where((key <= q_at) & (key < valid), s, LOW)
            new = jnp.maximum(top, jnp.max(s, axis=0, keepdims=True))
            p = jnp.exp2(s - new).astype(BF16)
            acc_ref[...] = acc_ref[...] * jnp.exp2(top - new) + dot_rows(vt_ref[m], p)
            return new

        lax.fori_loop(0, TILES, body, top)
        finish()


def attend_call(lengths, recv):
    vmem = pl.BlockSpec(memory_space=pltpu.VMEM)
    return pl.pallas_call(
        attend_kernel,
        in_specs=[pl.BlockSpec(memory_space=pltpu.SMEM), vmem],
        out_specs=[vmem, vmem],
        out_shape=[
            jax.ShapeDtypeStruct((DEVICES, 2, 256), BF16),
            jax.ShapeDtypeStruct((1, 1, GLOBALS * HEAD_DIM), BF16),
        ],
        scratch_shapes=[
            pltpu.VMEM((HEAD_DIM, QUERIES), BF16),
            pltpu.VMEM((COUNT, 128), BF16),
            pltpu.VMEM((TILES, VROWS, QT), BF16),
            pltpu.VMEM((512 + PAD, 128), F32),
            pltpu.VMEM((VROWS, QUERIES), F32),
        ],
        compiler_params=pltpu.CompilerParams(vmem_limit_bytes=32 * 2**20),
        name="attend",
    )(lengths, recv)


def output_kernel(back_ref, merged_ref, mixed_out_ref, out_ref, wide_ref, sum_ref):
    for h in range(HEADS):
        rows = mixed_out_ref[h * HEAD_DIM : (h + 1) * HEAD_DIM, :]
        for j in range(4):
            wide_ref[h * 128 + j * HEAD_DIM : h * 128 + (j + 1) * HEAD_DIM, :] = rows
    block = iota((2 * USERS, 128), 1) // HEAD_DIM
    keep = [(block == j).astype(F32).astype(BF16) for j in range(4)]
    parts = [[] for _ in range(8)]
    for h in range(HEADS):
        for t in range(2):
            x = back_ref[:, h, :, t * 128 : (t + 1) * 128].reshape(2 * USERS, 128)
            for j in range(4):
                parts[t * 4 + j].append(x * keep[j])
    lhs = jnp.concatenate([jnp.concatenate(p, axis=1) for p in parts], axis=0)
    prod = dot_rows(lhs, wide_ref[...])
    for c in range(4):
        cols = slice(c * 128, (c + 1) * 128)
        for i in range(8):
            rows = slice(i * 2 * USERS, (i + 1) * 2 * USERS)
            sum_ref[c, pl.ds(i, 2 * USERS, stride=8), :] = prod[rows, cols]
        out_ref[:, cols] = (merged_ref[:, cols].astype(F32) + sum_ref[c, : USERS * TOKENS]).astype(BF16)


def output_call(back, merged, mixed_out):
    vmem = pl.BlockSpec(memory_space=pltpu.VMEM)
    return pl.pallas_call(
        output_kernel,
        in_specs=[vmem] * 3,
        out_specs=vmem,
        out_shape=jax.ShapeDtypeStruct((USERS * TOKENS, WIDTH), BF16),
        scratch_shapes=[
            pltpu.VMEM((HEADS * 128, WIDTH), BF16),
            pltpu.VMEM((4, USERS * TOKENS + PAD, 128), F32),
        ],
        compiler_params=pltpu.CompilerParams(vmem_limit_bytes=16 * 2**20),
        name="output",
    )(back, merged, mixed_out)


def per_device(
    events,
    global_tokens,
    lengths,
    inner_qkv,
    inner_out,
    merge_gain,
    global_gain,
    mixed_qkv,
    mixed_out,
):
    merged, payload = inner_call(
        events,
        global_tokens.reshape(USERS, WIDTH),
        inner_qkv,
        inner_out,
        merge_gain.reshape(1, WIDTH),
        global_gain.reshape(1, WIDTH),
        mixed_qkv,
    )
    arrived = lax.all_to_all(
        payload.reshape(DEVICES, 2, 896), ("seq", "head"), split_axis=0, concat_axis=0, tiled=True
    )
    att, glob = attend_call(lengths, arrived)
    back = lax.all_to_all(att, ("seq", "head"), split_axis=0, concat_axis=0, tiled=True)
    out = output_call(back.reshape(USERS, HEADS, 2, 256), merged, mixed_out)
    return (out.reshape(USERS, TOKENS, WIDTH), glob)


def solution(mesh):
    in_specs = (
        P(None, ("seq", "head"), None),
        P(None, "seq", None),
        P(),
        P(),
        P(),
        P(),
        P(),
        P(),
        P(),
    )
    out_specs = (P(None, ("seq", "head"), None), P("seq", "head", None))
    return jax.shard_map(
        per_device, mesh=mesh, in_specs=in_specs, out_specs=out_specs, check_vma=False
    )
```
